32 devices in a mesh: gx: 4 (over z), gy: 4 (over y, x), gz: 2 (over core).
Axes of the slice: x: 2, y: 2, z: 4, core: 2. Of those that a mesh axis runs over, the one named last changes fastest.
Arguments:
- interact: bfloat16 [16, 8192, 512], P(None, ('gx', 'gy', 'gz')), may hold values from -6 to 6
- weight_one: bfloat16 [512, 1024], replicated, may hold values from -0.25 to 0.25
- bias_one: float32 [1024], replicated, may hold values from -3 to 3
- weight_two: bfloat16 [1024, 1024], replicated, may hold values from -0.1875 to 0.1875
- bias_two: float32 [1024], replicated, may hold values from -3 to 3
- weight_three: bfloat16 [1024, 512], replicated, may hold values from -0.1875 to 0.1875
- bias_three: float32 [512], replicated, may hold values from -3 to 3
- weight_four: bfloat16 [512, 256], replicated, may hold values from -0.25 to 0.25
- bias_four: float32 [256], replicated, may hold values from -3 to 3
- weight_out: bfloat16 [256, 1], replicated, may hold values from -1 to 1
- bias_out: float32 [1], replicated, may hold values from -1.5 to 0
- bucket_index: int32 [16, 8192], P(None, ('gx', 'gy', 'gz')), may hold values from 0 to 4095
- labels: int32 [16, 8192], P(None, ('gx', 'gy', 'gz')), may hold values from 0 to 1
Outputs:
- bucket_stats: float32 [16, 4, 4096], P(None, None, 'gx')
- summary: float32 [16, 4], replicated
The draws below stay inside these ranges and needn't reach their ends.
All inputs are finite; a program needn't handle non-finite values.
Results may differ from the reference program's by a relative error of at most 0.0045.
Values sent between devices are 32-bit elements; how exact they have to be, the bound alone decides.
A program may use at most 128 MiB of HBM per device.

```python
import jax
import jax.numpy as jnp
from jax import lax

DIN = 512
H1 = 1024
H2 = 1024
H3 = 512
H4 = 256
NBUCK = 4096
STEPS = 16
EXAMPLES = 8192


def label_and_bucket(key):
    base_key = jax.random.fold_in(key, 7103)
    subkeys = jax.random.split(base_key, 3)
    positions = jnp.arange(EXAMPLES, dtype=jnp.int32)[None, :]
    threshold = 100 + 300 * positions // EXAMPLES
    dice_roll = jax.random.randint(subkeys[0], (STEPS, EXAMPLES), 0, 1000, dtype=jnp.int32)
    clicked = (dice_roll < threshold).astype(jnp.int32)
    lower_draw = jax.random.randint(subkeys[1], (STEPS, EXAMPLES), 0, NBUCK, dtype=jnp.int32)
    upper_draw = jax.random.randint(subkeys[2], (STEPS, EXAMPLES), 0, NBUCK, dtype=jnp.int32)
    buckets = jnp.where(clicked == 1, jnp.maximum(lower_draw, upper_draw), lower_draw)
    return (clicked, buckets)


def draw_labels(key, part):
    return label_and_bucket(key)[0]


def draw_bucket_index(key, part):
    return label_and_bucket(key)[1]


def level_of(own_key, extent, cuts, low, top_value):
    factor_of = 1.0
    for position, blocks in cuts:
        draws = jax.random.uniform(jax.random.fold_in(jax.random.fold_in(own_key, 6), position), (blocks,), jnp.float32, low / len(cuts), top_value / len(cuts))
        factor_of = factor_of * jnp.repeat(jnp.exp(draws), extent[position] // blocks).reshape((-1,) + (1,) * (len(extent) - 1 - position))
    return factor_of


def scatter_about(stream_key, shape, spread, bound, shards=(), kind=jnp.bfloat16):
    gain = level_of(stream_key, shape, shards, -0.22, 0.18) if shards else 1.0
    array = jax.random.normal(stream_key, shape, jnp.float32) * spread * gain
    return jnp.minimum(jnp.maximum(array, -bound), bound).astype(kind)


def setup_inputs(seed: int = 0) -> dict:
    key_list = jax.random.split(jax.random.key(seed), 14)
    return {
        "interact": scatter_about(key_list[0], (STEPS, EXAMPLES, DIN), 1.0, 6.0, ((1, 32),)),
        "weight_one": scatter_about(key_list[1], (DIN, H1), DIN ** -0.5, 0.25),
        "bias_one": scatter_about(key_list[2], (H1,), 0.5, 3.0, (), jnp.float32),
        "weight_two": scatter_about(key_list[3], (H1, H2), H1 ** -0.5, 0.1875),
        "bias_two": scatter_about(key_list[4], (H2,), 0.5, 3.0, (), jnp.float32),
        "weight_three": scatter_about(key_list[5], (H2, H3), H2 ** -0.5, 0.1875),
        "bias_three": scatter_about(key_list[6], (H3,), 0.5, 3.0, (), jnp.float32),
        "weight_four": scatter_about(key_list[7], (H3, H4), H3 ** -0.5, 0.25),
        "bias_four": scatter_about(key_list[8], (H4,), 0.5, 3.0, (), jnp.float32),
        "weight_out": scatter_about(key_list[9], (H4, 1), 0.2, 1.0),
        "bias_out": jnp.clip(jax.random.uniform(key_list[10], (1,), jnp.float32, -1.5, 0.0), -1.5, 0.0),
        "bucket_index": draw_bucket_index(jax.random.fold_in(key_list[13], 71), 0),
        "labels": draw_labels(jax.random.fold_in(key_list[13], 71), 0),
    }


def layer_relu(inputs, weight, offset):
    return jax.nn.relu(jnp.dot(inputs, weight, preferred_element_type=jnp.float32) + offset).astype(jnp.bfloat16)


def bucket_reports(totals):
    positives = totals[:, 0]
    negatives = totals[:, 1]
    counts = jnp.maximum(positives + negatives, 1.0)
    return jnp.stack([positives / counts, totals[:, 2] / counts, totals[:, 3] / counts, totals[:, 4] / counts], axis=1)


def summarize(numerator, column_sums):
    pair_count = jnp.maximum(column_sums[:, 0] * column_sums[:, 1], 1.0)
    example_count = jnp.maximum(column_sums[:, 0] + column_sums[:, 1], 1.0)
    return jnp.stack([numerator / pair_count, column_sums[:, 3] / example_count,
                      column_sums[:, 2] / jnp.maximum(column_sums[:, 0], 1.0),
                      column_sums[:, 4] / example_count], axis=1)


def reference(interact, weight_one, bias_one, weight_two, bias_two, weight_three, bias_three,
              weight_four, bias_four, weight_out, bias_out, bucket_index, labels):
    def one_interval(inputs):
        features, buckets, targets = inputs
        hidden = layer_relu(features, weight_one, bias_one)
        hidden = layer_relu(hidden, weight_two, bias_two)
        hidden = layer_relu(hidden, weight_three, bias_three)
        hidden = layer_relu(hidden, weight_four, bias_four)
        logits = jnp.dot(hidden, weight_out, preferred_element_type=jnp.float32)[:, 0] + bias_out[0]
        observed = targets.astype(jnp.float32)
        predicted = jax.nn.sigmoid(logits)
        losses = jax.nn.softplus(logits) - observed * logits
        squared = (predicted - observed) ** 2
        values = jnp.stack([observed, 1.0 - observed, predicted, losses, squared], axis=1)
        return jax.ops.segment_sum(values, buckets, num_segments=NBUCK).T

    totals = lax.map(one_interval, (interact, bucket_index, labels))
    negatives = totals[:, 1]
    below_count = jnp.cumsum(negatives, axis=1) - negatives
    numerator = jnp.sum(totals[:, 0] * (below_count + 0.5 * negatives), axis=1)
    return bucket_reports(totals), summarize(numerator, jnp.sum(totals, axis=2))
```

```python
import functools

import jax
import jax.numpy as jnp
from jax import lax
from jax.experimental import pallas as pl
from jax.experimental.pallas import tpu as pltpu
from jax.sharding import PartitionSpec as P

NBUCK = 4096
LANES = 128
HIGHS = NBUCK // LANES
MESH = pl.DeviceIdType.MESH
AXES = ("gx", "gy", "gz")


def mlp_kernel(
    rows,
    x_ref,
    w1_ref,
    b1_ref,
    w2_ref,
    b2_ref,
    w3_ref,
    b3_ref,
    w4_ref,
    b4_ref,
    wo_ref,
    bo_ref,
    bucket_ref,
    label_ref,
    out_ref,
    h1_ref,
    h2_ref,
    h3_ref,
    h4_ref,
):
    step = pl.program_id(0)

    def layer(src, w_ref, b_ref, dst):
        for col in range(0, w_ref.shape[1], 256):
            cols = slice(col, col + 256)
            acc = jnp.dot(src[...], w_ref[:, cols], preferred_element_type=jnp.float32)
            dst[:, cols] = jnp.maximum(acc + b_ref[:, cols], 0.0).astype(jnp.bfloat16)

    layer(x_ref, w1_ref, b1_ref, h1_ref)
    layer(h1_ref, w2_ref, b2_ref, h2_ref)
    layer(h2_ref, w3_ref, b3_ref, h3_ref)
    layer(h3_ref, w4_ref, b4_ref, h4_ref)
    wide = jnp.broadcast_to(wo_ref[...].astype(jnp.float32), (16, wo_ref.shape[1]))
    logits = lax.dot_general(
        wide.astype(jnp.bfloat16),
        h4_ref[...],
        (((1,), (1,)), ((), ())),
        preferred_element_type=jnp.float32,
    )[0:1] + bo_ref[...]
    per = rows // LANES
    for row in range(x_ref.shape[0] // LANES):
        out_ref[step, 0, row : row + 1, :] = logits[:, row * LANES : (row + 1) * LANES]

    @pl.when(step == 0)
    def _():
        intervals, lines = bucket_ref.shape[0], out_ref.shape[2]
        for i in range(intervals):
            for j in range(per):
                slot, row = divmod(i * per + j, lines)
                cols = slice(j * LANES, (j + 1) * LANES)
                out_ref[slot, 1, row : row + 1, :] = bucket_ref[i : i + 1, cols].astype(
                    jnp.float32
                )
                out_ref[slot, 2, row : row + 1, :] = label_ref[i : i + 1, cols].astype(
                    jnp.float32
                )


def merge_kernel(
    sizes,
    slots,
    packed_ref,
    stats_ref,
    summary_ref,
    got,
    vals,
    hist,
    res,
    send_sem,
    recv_sem,
    res_send_sem,
    res_recv_sem,
):
    nx, ny, nz = sizes
    group = ny * nz
    devices = nx * group
    x, y, z = (lax.axis_index(a) for a in AXES)
    mine = y * nz + z
    me = x * group + mine
    slot = lax.rem(mine, slots)
    copies = mine // slots
    intervals = stats_ref.shape[0]
    held = intervals // slots
    blocks = stats_ref.shape[2]
    rows = packed_ref.shape[2]
    per = rows // held

    def place(d):
        inner = lax.rem(d, group)
        return (d // group, inner // nz, lax.rem(inner, nz))

    barrier = pltpu.get_barrier_semaphore()

    @pl.loop(1, devices)
    def _(k):
        d = lax.rem(me + k, devices)
        pl.semaphore_signal(barrier, inc=1, device_id=place(d), device_id_type=MESH)

    pl.semaphore_wait(barrier, devices - 1)

    @pl.loop(1, devices)
    def _(k):
        d = lax.rem(me + k, devices)
        pltpu.make_async_remote_copy(
            src_ref=packed_ref.at[lax.rem(lax.rem(d, group), slots)],
            dst_ref=got.at[me],
            send_sem=send_sem,
            recv_sem=recv_sem,
            device_id=place(d),
            device_id_type=MESH,
        ).start()

    pltpu.make_async_copy(packed_ref.at[slot], got.at[me], recv_sem).start()
    pltpu.make_async_copy(got, got, recv_sem).wait()

    logit = got[:, 0]
    label = got[:, 2]
    small = jnp.exp(-jnp.abs(logit))
    predicted = jnp.where(logit >= 0.0, 1.0, small) / (1.0 + small)
    losses = jnp.maximum(logit, 0.0) + jnp.log1p(small) - label * logit
    squared = (predicted - label) ** 2
    vals[:, 0] = predicted
    vals[:, 1] = losses
    vals[:, 2] = squared

    width = per * LANES
    low_ids = lax.broadcasted_iota(jnp.int32, (LANES, width), 0)
    high_ids = lax.broadcasted_iota(jnp.int32, (HIGHS, width), 0)
    block_ids = lax.broadcasted_iota(jnp.int32, (blocks, width), 0) + x * blocks
    tall = 2 * HIGHS + 6 * blocks

    def add(n, totals):
        out = []
        for i in range(held):
            def line(ref, k):
                return jnp.concatenate(
                    [ref[n, k, i * per + j : i * per + j + 1, :] for j in range(per)], axis=1
                )

            bucket = line(got, 1).astype(jnp.int32)
            observed = line(got, 2)
            low = bucket & (LANES - 1)
            high = lax.shift_right_logical(bucket, LANES.bit_length() - 1)
            one_hot = jnp.where(low_ids == low, 1.0, 0.0).astype(jnp.bfloat16)
            at_high = high_ids == high
            at_block = block_ids == high
            parts = [
                jnp.where(at_high, observed, 0.0),
                jnp.where(at_high, 1.0 - observed, 0.0),
            ]
            lower = []
            for k in range(3):
                value = line(vals, k)
                upper = value.astype(jnp.bfloat16).astype(jnp.float32)
                parts.append(jnp.where(at_block, upper, 0.0))
                lower.append(jnp.where(at_block, value - upper, 0.0))
            left = jnp.concatenate(parts + lower, axis=0).astype(jnp.bfloat16)
            out.append(
                totals[i]
                + lax.dot_general(
                    left, one_hot, (((1,), (1,)), ((), ())), preferred_element_type=jnp.float32
                )
            )
        return tuple(out)

    zero = jnp.zeros((tall, LANES), jnp.float32)
    totals = lax.fori_loop(0, devices, add, (zero,) * held)

    before = lax.broadcasted_iota(jnp.int32, (LANES, LANES), 0)
    after = lax.broadcasted_iota(jnp.int32, (LANES, LANES), 1)
    lane_before = jnp.where(before < after, 1.0, 0.0)
    row_before = jnp.where(
        lax.broadcasted_iota(jnp.int32, (HIGHS, HIGHS), 0)
        > lax.broadcasted_iota(jnp.int32, (HIGHS, HIGHS), 1),
        1.0,
        0.0,
    )
    lane_ids = lax.broadcasted_iota(jnp.int32, (8, LANES), 1)
    exact = functools.partial(
        jnp.dot, preferred_element_type=jnp.float32, precision=lax.Precision.HIGHEST
    )

    def whole_sum(a):
        return jnp.sum(jnp.sum(a, axis=0, keepdims=True), axis=1, keepdims=True)

    for i in range(held):
        total = totals[i]
        hist[...] = total[: 2 * HIGHS]
        own = pl.ds(pl.multiple_of(x * blocks, blocks), blocks)
        own_neg = pl.ds(pl.multiple_of(HIGHS + x * blocks, blocks), blocks)
        positives, negatives = hist[own, :], hist[own_neg, :]
        count = jnp.maximum(positives + negatives, 1.0)
        at = slot * held + i
        res[at, 0:blocks, :] = positives / count
        for k in range(3):
            first = 2 * HIGHS + k * blocks
            second = first + 3 * blocks
            value = total[first : first + blocks] + total[second : second + blocks]
            res[at, (k + 1) * blocks : (k + 2) * blocks, :] = value / count
        pos, neg = total[:HIGHS], total[HIGHS : 2 * HIGHS]
        rows_below = jnp.sum(exact(row_before, neg), axis=1, keepdims=True)
        below = exact(neg, lane_before) + rows_below
        numerator = whole_sum(pos * (below + 0.5 * neg))
        p_sum, n_sum = whole_sum(pos), whole_sum(neg)
        sums = []
        for k in range(3):
            part = jnp.sum(vals[:, k, i * per : (i + 1) * per, :], axis=0)
            sums.append(whole_sum(part))
        examples = jnp.maximum(p_sum + n_sum, 1.0)
        line = jnp.where(lane_ids == 0, numerator / jnp.maximum(p_sum * n_sum, 1.0), 0.0)
        line = jnp.where(lane_ids == 1, sums[1] / examples, line)
        line = jnp.where(lane_ids == 2, sums[0] / jnp.maximum(p_sum, 1.0), line)
        line = jnp.where(lane_ids == 3, sums[2] / examples, line)
        res[at, 4 * blocks : 4 * blocks + 8, :] = line

    here = pl.ds(slot * held, held)

    @pl.loop(1, slots)
    def _(k):
        d = x * group + copies * slots + lax.rem(slot + k, slots)
        pltpu.make_async_remote_copy(
            src_ref=res.at[here],
            dst_ref=res.at[here],
            send_sem=res_send_sem,
            recv_sem=res_recv_sem,
            device_id=place(d),
            device_id_type=MESH,
        ).start()

    others = res.at[pl.ds(0, intervals - held)]
    if slots > 1:
        pltpu.make_async_copy(others, others, res_recv_sem).wait()
    for k in range(4):
        stats_ref[:, k] = res[:, k * blocks : (k + 1) * blocks, :]
    summary_ref[...] = res[:, 4 * blocks : 4 * blocks + 8, :]
    if slots > 1:
        pltpu.make_async_copy(others, others, res_send_sem).wait()
    if devices > 1:
        sent = got.at[pl.ds(0, devices - 1)]
        pltpu.make_async_copy(sent, sent, send_sem).wait()


def on_device(
    sizes,
    interact,
    weight_one,
    bias_one,
    weight_two,
    bias_two,
    weight_three,
    bias_three,
    weight_four,
    bias_four,
    weight_out,
    bias_out,
    bucket_index,
    labels,
):
    intervals, rows, features = interact.shape
    nx, ny, nz = sizes
    devices = nx * ny * nz
    slots = min(ny * nz, intervals)
    held = intervals // slots
    tile = held * rows
    lines = tile // LANES
    blocks = HIGHS // nx
    flat = interact.reshape(intervals * rows, features)
    wide = [w.shape[1] for w in (weight_one, weight_two, weight_three, weight_four)]

    def whole(a):
        return pl.BlockSpec(a.shape, lambda s: (0,) * a.ndim)

    operands = [
        weight_one,
        bias_one.reshape(1, -1),
        weight_two,
        bias_two.reshape(1, -1),
        weight_three,
        bias_three.reshape(1, -1),
        weight_four,
        bias_four.reshape(1, -1),
        weight_out.reshape(1, -1),
        bias_out.reshape(1, 1),
        bucket_index,
        labels,
    ]
    packed = pl.pallas_call(
        functools.partial(mlp_kernel, rows),
        grid=(slots,),
        in_specs=[pl.BlockSpec((tile, features), lambda s: (s, 0))]
        + [whole(a) for a in operands],
        out_specs=pl.BlockSpec((slots, 3, lines, LANES), lambda s: (0, 0, 0, 0)),
        out_shape=jax.ShapeDtypeStruct((slots, 3, lines, LANES), jnp.float32),
        scratch_shapes=[pltpu.VMEM((tile, w), jnp.bfloat16) for w in wide],
        compiler_params=pltpu.CompilerParams(vmem_limit_bytes=40 * 2**20),
        name="top_mlp",
    )(flat, *operands)

    vmem = pl.BlockSpec(memory_space=pltpu.VMEM)
    stats, summary = pl.pallas_call(
        functools.partial(merge_kernel, sizes, slots),
        in_specs=[vmem],
        out_specs=[vmem, vmem],
        out_shape=[
            jax.ShapeDtypeStruct((intervals, 4, blocks, LANES), jnp.float32),
            jax.ShapeDtypeStruct((intervals, 8, LANES), jnp.float32),
        ],
        scratch_shapes=[
            pltpu.VMEM((devices, 3, lines, LANES), jnp.float32),
            pltpu.VMEM((devices, 3, lines, LANES), jnp.float32),
            pltpu.VMEM((2 * HIGHS, LANES), jnp.float32),
            pltpu.VMEM((intervals, 4 * blocks + 8, LANES), jnp.float32),
            pltpu.SemaphoreType.DMA,
            pltpu.SemaphoreType.DMA,
            pltpu.SemaphoreType.DMA,
            pltpu.SemaphoreType.DMA,
        ],
        compiler_params=pltpu.CompilerParams(
            collective_id=0, has_side_effects=True, vmem_limit_bytes=24 * 2**20
        ),
        name="merge_buckets",
    )(packed)
    return stats.reshape(intervals, 4, blocks * LANES), summary[:, 0, :4]


def solution(mesh):
    sizes = tuple(mesh.shape[a] for a in AXES)
    in_specs = (
        (P(None, AXES, None),) + (P(),) * 10 + (P(None, AXES), P(None, AXES))
    )
    out_specs = (P(None, None, "gx"), P())
    return jax.shard_map(
        functools.partial(on_device, sizes),
        mesh=mesh,
        in_specs=in_specs,
        out_specs=out_specs,
        check_vma=False,
    )
```

```python
import functools

import jax
import jax.numpy as jnp
from jax import lax
from jax.experimental import pallas as pl
from jax.experimental.pallas import tpu as pltpu
from jax.sharding import PartitionSpec as P

NBUCK = 4096
LANES = 128
PAIR = 2
HIGHS = NBUCK // LANES
MESH = pl.DeviceIdType.MESH
AXES = ("gx", "gy", "gz")


def exact_digits(a, bound):
    digits, scale = [], 1.0
    while True:
        if bound <= 256:
            return digits + [(a, scale)]
        upper = jnp.floor(a * (1.0 / 256.0))
        digits.append((a - 256.0 * upper, scale))
        a, bound, scale = upper, bound // 256, scale * 256.0


def report_kernel(
    sizes,
    slots,
    x_hbm,
    w1_hbm,
    b1_hbm,
    w2_hbm,
    b2_hbm,
    w3_hbm,
    b3_hbm,
    w4_hbm,
    b4_hbm,
    wo_hbm,
    bo_ref,
    bucket_hbm,
    label_hbm,
    stats_ref,
    summary_ref,
    x_ref,
    w1_ref,
    b1_ref,
    w2_ref,
    b2_ref,
    w3_ref,
    b3_ref,
    w4_ref,
    b4_ref,
    wo_ref,
    bucket_ref,
    label_ref,
    hidden_one,
    hidden_two,
    hidden_three,
    hidden_four,
    packed,
    got,
    vals,
    hist,
    res,
    x_sem,
    w_sem,
    send_sem,
    recv_sem,
    res_send_sem,
    res_recv_sem,
):
    nx, ny, nz = sizes
    group = ny * nz
    devices = nx * group
    x, y, z = (lax.axis_index(a) for a in AXES)
    mine = y * nz + z
    me = x * group + mine
    slot = lax.rem(mine, slots)
    own_copy = mine // slots
    copies = group // slots
    intervals = stats_ref.shape[0]
    held = intervals // slots
    blocks = stats_ref.shape[2]
    tile = x_ref.shape[1]
    lines = tile // LANES
    per = lines // held

    def place(d):
        inner = lax.rem(d, group)
        return (d // group, inner // nz, lax.rem(inner, nz))

    def turn(i):
        return lax.rem(slot + 1 + i, slots)

    loads = {}
    pairs = (
        ("w1", w1_hbm, w1_ref),
        ("b1", b1_hbm, b1_ref),
        ("w2", w2_hbm, w2_ref),
        ("b2", b2_hbm, b2_ref),
        ("w3", w3_hbm, w3_ref),
        ("b3", b3_hbm, b3_ref),
        ("w4", w4_hbm, w4_ref),
        ("b4", b4_hbm, b4_ref),
        ("wo", wo_hbm, wo_ref),
        ("bucket", bucket_hbm, bucket_ref),
        ("label", label_hbm, label_ref),
    )

    def x_load(i):
        at = turn(i)
        return pltpu.make_async_copy(x_hbm.at[at], x_ref.at[at], x_sem.at[i])

    x_load(0).start()
    for k, (key, src, dst) in enumerate(pairs):
        loads[key] = pltpu.make_async_copy(src, dst, w_sem.at[k])
        loads[key].start()
        if key == "b1":
            for i in range(1, PAIR if slots % PAIR == 0 else 1):
                x_load(i).start()
    for i in range(PAIR if slots % PAIR == 0 else 1, slots):
        x_load(i).start()

    barrier = pltpu.get_barrier_semaphore()

    @pl.loop(1, devices)
    def _(k):
        d = lax.rem(me + k, devices)
        pl.semaphore_signal(barrier, inc=1, device_id=place(d), device_id_type=MESH)

    def layer(src, w_ref, b_ref, dst):
        for col in range(0, w_ref.shape[1], 256):
            cols = slice(col, col + 256)
            acc = jnp.dot(src[...], w_ref[:, cols], preferred_element_type=jnp.float32)
            dst[:, cols] = jnp.maximum(acc + b_ref[:, cols], 0.0).astype(jnp.bfloat16)

    def scores(order, first):
        def need(*keys):
            if first:
                for key in keys:
                    loads[key].wait()

        where = [turn(i) for i in order]
        for i in order:
            x_load(i).wait()
        need("w1", "b1")
        for p, c in enumerate(where):
            layer(x_ref.at[c], w1_ref, b1_ref, hidden_one.at[p])
        need("w2", "b2")
        for p, c in enumerate(where):
            layer(hidden_one.at[p], w2_ref, b2_ref, hidden_two.at[p])
        need("w3", "b3")
        for p, c in enumerate(where):
            layer(hidden_two.at[p], w3_ref, b3_ref, hidden_three.at[p])
        need("w4", "b4")
        for p, c in enumerate(where):
            layer(hidden_three.at[p], w4_ref, b4_ref, hidden_four.at[p])
        need("wo")
        wide = jnp.broadcast_to(wo_ref[...].astype(jnp.float32), (16, wo_ref.shape[1]))
        for p, c in enumerate(where):
            logits = lax.dot_general(
                wide.astype(jnp.bfloat16),
                hidden_four[p],
                (((1,), (1,)), ((), ())),
                preferred_element_type=jnp.float32,
            )[0:1] + bo_ref[0]
            for row in range(lines):
                packed[c, 0, row : row + 1, :] = logits[:, row * LANES : (row + 1) * LANES]

    def send(c):
        here = x * copies + own_copy
        for k in range(nx * copies):
            rep = lax.rem(here + k, nx * copies)
            inner = lax.rem(rep, copies) * slots + c
            remote = pltpu.make_async_remote_copy(
                src_ref=packed.at[c],
                dst_ref=got.at[me],
                send_sem=send_sem,
                recv_sem=recv_sem,
                device_id=(rep // copies, inner // nz, lax.rem(inner, nz)),
                device_id_type=MESH,
            )
            if k == 0:
                pl.when(c != slot)(remote.start)
            else:
                remote.start()

    pair = PAIR if slots % PAIR == 0 else 1
    scores(range(pair), True)

    loads["bucket"].wait()
    loads["label"].wait()
    for i in range(intervals):
        for j in range(per):
            c, row = divmod(i * per + j, lines)
            cols = slice(j * LANES, (j + 1) * LANES)
            packed[c, 1, row : row + 1, :] = bucket_ref[i : i + 1, cols].astype(jnp.float32)
            packed[c, 2, row : row + 1, :] = label_ref[i : i + 1, cols].astype(jnp.float32)

    pl.semaphore_wait(barrier, devices - 1)
    for i in range(pair):
        send(turn(i))

    @pl.loop(1, slots // pair)
    def _(step):
        order = [step * pair + p for p in range(pair)]
        scores(order, False)
        for i in order:
            send(turn(i))

    pltpu.make_async_copy(packed.at[slot], got.at[me], recv_sem).start()
    pltpu.make_async_copy(got, got, recv_sem).wait()

    logit = got[:, 0]
    label = got[:, 2]
    small = jnp.exp(-jnp.abs(logit))
    predicted = jnp.where(logit >= 0.0, 1.0, small) / (1.0 + small)
    losses = jnp.maximum(logit, 0.0) + jnp.log1p(small) - label * logit
    squared = (predicted - label) ** 2
    vals[:, 0] = predicted
    vals[:, 1] = losses
    vals[:, 2] = squared

    batch = next(b for b in (8, 4, 2, 1) if devices % b == 0)
    width = batch * per * LANES
    low_ids = lax.broadcasted_iota(jnp.int32, (LANES, width), 0)
    high_ids = lax.broadcasted_iota(jnp.int32, (HIGHS, width), 0)
    block_ids = lax.broadcasted_iota(jnp.int32, (blocks, width), 0) + x * blocks
    tall = 2 * HIGHS + 6 * blocks

    def add(step, totals):
        out = []
        for i in range(held):

            def line(ref, k):
                return jnp.concatenate(
                    [
                        ref[step * batch + n, k, row : row + 1, :]
                        for n in range(batch)
                        for row in range(i * per, (i + 1) * per)
                    ],
                    axis=1,
                )

            bucket = line(got, 1).astype(jnp.int32)
            observed = line(got, 2)
            low = bucket & (LANES - 1)
            high = lax.shift_right_logical(bucket, LANES.bit_length() - 1)
            one_hot = jnp.where(low_ids == low, 1.0, 0.0).astype(jnp.bfloat16)
            at_high = high_ids == high
            at_block = block_ids == high
            parts = [
                jnp.where(at_high, observed, 0.0),
                jnp.where(at_high, 1.0 - observed, 0.0),
            ]
            lower = []
            for k in range(3):
                value = line(vals, k)
                upper = value.astype(jnp.bfloat16).astype(jnp.float32)
                parts.append(jnp.where(at_block, upper, 0.0))
                lower.append(jnp.where(at_block, value - upper, 0.0))
            left = jnp.concatenate(parts + lower, axis=0).astype(jnp.bfloat16)
            out.append(
                totals[i]
                + lax.dot_general(
                    left, one_hot, (((1,), (1,)), ((), ())), preferred_element_type=jnp.float32
                )
            )
        return tuple(out)

    zero = jnp.zeros((tall, LANES), jnp.float32)
    totals = lax.fori_loop(0, devices // batch, add, (zero,) * held)

    def below_than(size, lower_first):
        a = lax.broadcasted_iota(jnp.int32, (size, size), 0)
        b = lax.broadcasted_iota(jnp.int32, (size, size), 1)
        return jnp.where(a < b if lower_first else b < a, 1.0, 0.0).astype(jnp.bfloat16)

    lane_before = below_than(LANES, True)
    row_before = below_than(HIGHS, False)
    lane_ids = lax.broadcasted_iota(jnp.int32, (8, LANES), 1)
    bound = devices * per * LANES

    for i in range(held):
        total = totals[i]
        at = slot * held + i
        hist[...] = total[: 2 * HIGHS]
        own = pl.ds(pl.multiple_of(x * blocks, blocks), blocks)
        own_neg = pl.ds(pl.multiple_of(HIGHS + x * blocks, blocks), blocks)
        positives, negatives = hist[own, :], hist[own_neg, :]
        count = jnp.maximum(positives + negatives, 1.0)
        res[at, 0:blocks, :] = positives / count
        for k in range(3):
            first = 2 * HIGHS + k * blocks
            second = first + 3 * blocks
            value = total[first : first + blocks] + total[second : second + blocks]
            res[at, (k + 1) * blocks : (k + 2) * blocks, :] = value / count
        pos, neg = total[:HIGHS], total[HIGHS : 2 * HIGHS]
        lane_below = jnp.zeros((HIGHS, LANES), jnp.float32)
        rows_below = jnp.zeros((HIGHS, LANES), jnp.float32)
        for digit, scale in exact_digits(neg, bound):
            digit = digit.astype(jnp.bfloat16)
            lane_below += scale * jnp.dot(
                digit, lane_before, preferred_element_type=jnp.float32
            )
            rows_below += scale * jnp.dot(
                row_before, digit, preferred_element_type=jnp.float32
            )
        below = lane_below + jnp.sum(rows_below, axis=1, keepdims=True)
        sums = [pos * (below + 0.5 * neg), pos, neg]
        sums = [jnp.sum(a, axis=0, keepdims=True) for a in sums]
        for k in range(3):
            part = jnp.sum(vals[:, k, i * per : (i + 1) * per, :], axis=0)
            sums.append(jnp.sum(part, axis=0, keepdims=True))
        sums += [jnp.zeros((1, LANES), jnp.float32)] * 2
        sums = jnp.sum(jnp.concatenate(sums, axis=0), axis=1, keepdims=True)
        numerator, p_sum, n_sum, s_p, s_loss, s_sq = (sums[k : k + 1] for k in range(6))
        examples = jnp.maximum(p_sum + n_sum, 1.0)
        line = jnp.where(lane_ids == 0, numerator / jnp.maximum(p_sum * n_sum, 1.0), 0.0)
        line = jnp.where(lane_ids == 1, s_loss / examples, line)
        line = jnp.where(lane_ids == 2, s_p / jnp.maximum(p_sum, 1.0), line)
        line = jnp.where(lane_ids == 3, s_sq / examples, line)
        res[at, 4 * blocks : 4 * blocks + 8, :] = line

    here = pl.ds(slot * held, held)

    @pl.loop(1, slots)
    def _(k):
        d = x * group + own_copy * slots + lax.rem(slot + k, slots)
        pltpu.make_async_remote_copy(
            src_ref=res.at[here],
            dst_ref=res.at[here],
            send_sem=res_send_sem,
            recv_sem=res_recv_sem,
            device_id=place(d),
            device_id_type=MESH,
        ).start()

    others = res.at[pl.ds(0, intervals - held)]
    if slots > 1:
        pltpu.make_async_copy(others, others, res_recv_sem).wait()
    for k in range(4):
        stats_ref[:, k] = res[:, k * blocks : (k + 1) * blocks, :]
    summary_ref[...] = res[:, 4 * blocks : 4 * blocks + 8, :]
    if slots > 1:
        pltpu.make_async_copy(others, others, res_send_sem).wait()
    if devices > 1:
        sent = got.at[pl.ds(0, devices - 1)]
        pltpu.make_async_copy(sent, sent, send_sem).wait()


def on_device(sizes, *args):
    (
        interact,
        weight_one,
        bias_one,
        weight_two,
        bias_two,
        weight_three,
        bias_three,
        weight_four,
        bias_four,
        weight_out,
        bias_out,
        bucket_index,
        labels,
    ) = args
    intervals, rows, features = interact.shape
    nx, ny, nz = sizes
    devices = nx * ny * nz
    slots = min(ny * nz, intervals)
    pair = PAIR if slots % PAIR == 0 else 1
    held = intervals // slots
    tile = held * rows
    lines = tile // LANES
    blocks = HIGHS // nx
    weights = (weight_one, weight_two, weight_three, weight_four)
    operands = [
        interact.reshape(slots, tile, features),
        weight_one,
        bias_one.reshape(1, -1),
        weight_two,
        bias_two.reshape(1, -1),
        weight_three,
        bias_three.reshape(1, -1),
        weight_four,
        bias_four.reshape(1, -1),
        weight_out.reshape(1, -1),
        bias_out,
        bucket_index,
        labels,
    ]
    vmem = pl.BlockSpec(memory_space=pltpu.VMEM)
    in_specs = [pl.BlockSpec(memory_space=pltpu.HBM)] * len(operands)
    in_specs[10] = pl.BlockSpec(memory_space=pltpu.SMEM)
    stats, summary = pl.pallas_call(
        functools.partial(report_kernel, sizes, slots),
        in_specs=in_specs,
        out_specs=[vmem, vmem],
        out_shape=[
            jax.ShapeDtypeStruct((intervals, 4, blocks, LANES), jnp.float32),
            jax.ShapeDtypeStruct((intervals, 8, LANES), jnp.float32),
        ],
        scratch_shapes=[pltpu.VMEM(a.shape, a.dtype) for k, a in enumerate(operands) if k != 10]
        + [pltpu.VMEM((pair, tile, w.shape[1]), jnp.bfloat16) for w in weights]
        + [
            pltpu.VMEM((slots, 3, lines, LANES), jnp.float32),
            pltpu.VMEM((devices, 3, lines, LANES), jnp.float32),
            pltpu.VMEM((devices, 3, lines, LANES), jnp.float32),
            pltpu.VMEM((2 * HIGHS, LANES), jnp.float32),
            pltpu.VMEM((intervals, 4 * blocks + 8, LANES), jnp.float32),
            pltpu.SemaphoreType.DMA((slots,)),
            pltpu.SemaphoreType.DMA((11,)),
            pltpu.SemaphoreType.DMA,
            pltpu.SemaphoreType.DMA,
            pltpu.SemaphoreType.DMA,
            pltpu.SemaphoreType.DMA,
        ],
        compiler_params=pltpu.CompilerParams(
            collective_id=0, has_side_effects=True, vmem_limit_bytes=56 * 2**20
        ),
        name="report",
    )(*operands)
    return stats.reshape(intervals, 4, blocks * LANES), summary[:, 0, :4]


def solution(mesh):
    sizes = tuple(mesh.shape[a] for a in AXES)
    in_specs = (
        (P(None, AXES, None),) + (P(),) * 10 + (P(None, AXES), P(None, AXES))
    )
    out_specs = (P(None, None, "gx"), P())
    return jax.shard_map(
        functools.partial(on_device, sizes),
        mesh=mesh,
        in_specs=in_specs,
        out_specs=out_specs,
        check_vma=False,
    )
```

```python
import functools

import jax
import jax.numpy as jnp
from jax import lax
from jax.experimental import pallas as pl
from jax.experimental.pallas import tpu as pltpu
from jax.sharding import PartitionSpec as P

NBUCK = 4096
LANES = 128
PAIR = 2
HIGHS = NBUCK // LANES
MESH = pl.DeviceIdType.MESH
AXES = ("gx", "gy", "gz")


def exact_digits(a, bound):
    digits, scale = [], 1.0
    while True:
        if bound <= 256:
            return digits + [(a, scale)]
        upper = jnp.floor(a * (1.0 / 256.0))
        digits.append((a - 256.0 * upper, scale))
        a, bound, scale = upper, bound // 256, scale * 256.0


def report_kernel(
    sizes,
    slots,
    x_hbm,
    w1_hbm,
    b1_hbm,
    w2_hbm,
    b2_hbm,
    w3_hbm,
    b3_hbm,
    w4_hbm,
    b4_hbm,
    wo_hbm,
    bo_ref,
    bucket_hbm,
    label_hbm,
    stats_ref,
    summary_ref,
    x_ref,
    w1_ref,
    b1_ref,
    w2_ref,
    b2_ref,
    w3_ref,
    b3_ref,
    w4_ref,
    b4_ref,
    wo_ref,
    bucket_ref,
    label_ref,
    hidden_one,
    hidden_two,
    hidden_three,
    hidden_four,
    packed,
    got,
    vals,
    totals,
    res,
    x_sem,
    w_sem,
    send_sem,
    recv_sem,
    res_send_sem,
    res_recv_sem,
    out_sem,
):
    nx, ny, nz = sizes
    group = ny * nz
    devices = nx * group
    x, y, z = (lax.axis_index(a) for a in AXES)
    mine = y * nz + z
    me = x * group + mine
    slot = lax.rem(mine, slots)
    own_copy = mine // slots
    copies = group // slots
    intervals = stats_ref.shape[0]
    held = intervals // slots
    span = stats_ref.shape[2]
    blocks = span // LANES
    tile = x_ref.shape[1]
    lines = tile // LANES
    per = lines // held
    reps = nx * copies
    here = x * copies + own_copy
    pair = PAIR if slots % PAIR == 0 else 1

    def place(d):
        inner = lax.rem(d, group)
        return (d // group, inner // nz, lax.rem(inner, nz))

    def turn(i):
        return lax.rem(slot + 1 + i, slots)

    loads = {}
    pairs = (
        ("w1", w1_hbm, w1_ref),
        ("b1", b1_hbm, b1_ref),
        ("w2", w2_hbm, w2_ref),
        ("b2", b2_hbm, b2_ref),
        ("w3", w3_hbm, w3_ref),
        ("b3", b3_hbm, b3_ref),
        ("w4", w4_hbm, w4_ref),
        ("b4", b4_hbm, b4_ref),
        ("wo", wo_hbm, wo_ref),
        ("bucket", bucket_hbm, bucket_ref),
        ("label", label_hbm, label_ref),
    )

    def x_load(i):
        at = turn(i)
        return pltpu.make_async_copy(x_hbm.at[at], x_ref.at[at], x_sem.at[i])

    x_load(0).start()
    for k, (key, src, dst) in enumerate(pairs):
        loads[key] = pltpu.make_async_copy(src, dst, w_sem.at[k])
        loads[key].start()
        if key == "b1":
            for i in range(1, PAIR if slots % PAIR == 0 else 1):
                x_load(i).start()
    for i in range(PAIR if slots % PAIR == 0 else 1, slots):
        x_load(i).start()

    barrier = pltpu.get_barrier_semaphore()

    @pl.loop(1, devices)
    def _(k):
        d = lax.rem(me + k, devices)
        pl.semaphore_signal(barrier, inc=1, device_id=place(d), device_id_type=MESH)

    def layer(src, w_ref, b_ref, dst):
        for col in range(0, w_ref.shape[1], 256):
            cols = slice(col, col + 256)
            acc = jnp.dot(src[...], w_ref[:, cols], preferred_element_type=jnp.float32)
            dst[:, cols] = jnp.maximum(acc + b_ref[:, cols], 0.0).astype(jnp.bfloat16)

    def scores(order, first, beside=()):
        def need(*keys):
            if first:
                for key in keys:
                    loads[key].wait()

        where = [turn(i) for i in order]
        for i in order:
            x_load(i).wait()
        need("w1", "b1")
        for p, c in enumerate(where):
            layer(x_ref.at[c], w1_ref, b1_ref, hidden_one.at[p])
        need("w2", "b2")
        for p, c in enumerate(where):
            if p == len(where) - 1:
                for i in beside:
                    arrived(i)
            layer(hidden_one.at[p], w2_ref, b2_ref, hidden_two.at[p])
            if p == len(where) - 1:
                for i in beside:
                    add(i)
        need("w3", "b3")
        for p, c in enumerate(where):
            layer(hidden_two.at[p], w3_ref, b3_ref, hidden_three.at[p])
        need("w4", "b4")
        for p, c in enumerate(where):
            layer(hidden_three.at[p], w4_ref, b4_ref, hidden_four.at[p])
        need("wo")
        wide = jnp.broadcast_to(wo_ref[...].astype(jnp.float32), (16, wo_ref.shape[1]))
        for p, c in enumerate(where):
            logits = lax.dot_general(
                wide.astype(jnp.bfloat16),
                hidden_four[p],
                (((1,), (1,)), ((), ())),
                preferred_element_type=jnp.float32,
            )[0:1] + bo_ref[0]
            for row in range(lines):
                packed[c, 0, row : row + 1, :] = logits[:, row * LANES : (row + 1) * LANES]

    def send(i):
        c = turn(i)
        for k in range(reps):
            rep = lax.rem(here + k, reps)
            inner = lax.rem(rep, copies) * slots + c
            remote = pltpu.make_async_remote_copy(
                src_ref=packed.at[c],
                dst_ref=got.at[i, here],
                send_sem=send_sem.at[i],
                recv_sem=recv_sem.at[i],
                device_id=(rep // copies, inner // nz, lax.rem(inner, nz)),
                device_id_type=MESH,
            )
            if k == 0:
                pl.when(c != slot)(remote.start)
            else:
                remote.start()

    def arrived(i):
        pltpu.make_async_copy(got.at[i], got.at[i], recv_sem.at[i]).wait()

    width = reps * per * LANES
    low_ids = lax.broadcasted_iota(jnp.int32, (LANES, width), 0)
    high_ids = lax.broadcasted_iota(jnp.int32, (HIGHS, width), 0)
    block_ids = lax.broadcasted_iota(jnp.int32, (blocks, width), 0) + x * blocks

    def add(i):
        logit = got[i, :, 0]
        label = got[i, :, 2]
        small = jnp.exp(-jnp.abs(logit))
        predicted = jnp.where(logit >= 0.0, 1.0, small) / (1.0 + small)
        vals[i, :, 0] = predicted
        vals[i, :, 1] = jnp.maximum(logit, 0.0) + jnp.log1p(small) - label * logit
        vals[i, :, 2] = (predicted - label) ** 2
        for e in range(held):

            def line(ref, k):
                return jnp.concatenate(
                    [
                        ref[i, n, k, row : row + 1, :]
                        for n in range(reps)
                        for row in range(e * per, (e + 1) * per)
                    ],
                    axis=1,
                )

            bucket = line(got, 1).astype(jnp.int32)
            observed = line(got, 2)
            low = bucket & (LANES - 1)
            high = lax.shift_right_logical(bucket, LANES.bit_length() - 1)
            one_hot = jnp.where(low_ids == low, 1.0, 0.0).astype(jnp.bfloat16)
            at_high = high_ids == high
            at_block = block_ids == high
            parts = [
                jnp.where(at_high, observed, 0.0),
                jnp.where(at_high, 1.0 - observed, 0.0),
            ]
            lower = []
            for k in range(3):
                value = line(vals, k)
                upper = value.astype(jnp.bfloat16).astype(jnp.float32)
                parts.append(jnp.where(at_block, upper, 0.0))
                lower.append(jnp.where(at_block, value - upper, 0.0))
            left = jnp.concatenate(parts + lower, axis=0).astype(jnp.bfloat16)
            totals[e] += lax.dot_general(
                left, one_hot, (((1,), (1,)), ((), ())), preferred_element_type=jnp.float32
            )

    totals[...] = jnp.zeros_like(totals)
    scores(range(pair), True)

    loads["bucket"].wait()
    loads["label"].wait()
    for i in range(intervals):
        for j in range(per):
            c, row = divmod(i * per + j, lines)
            cols = slice(j * LANES, (j + 1) * LANES)
            packed[c, 1, row : row + 1, :] = bucket_ref[i : i + 1, cols].astype(jnp.float32)
            packed[c, 2, row : row + 1, :] = label_ref[i : i + 1, cols].astype(jnp.float32)

    pl.semaphore_wait(barrier, devices - 1)
    for i in range(pair):
        send(i)

    @pl.loop(1, slots // pair)
    def _(step):
        order = [step * pair + p for p in range(pair)]
        scores(order, False, [i - pair for i in order])
        for i in order:
            send(i)

    last = slots - 1
    pltpu.make_async_copy(packed.at[slot], got.at[last, here], recv_sem.at[last]).start()
    for i in range(slots - pair, slots):
        arrived(i)
        add(i)

    def below_than(size, lower_first):
        a = lax.broadcasted_iota(jnp.int32, (size, size), 0)
        b = lax.broadcasted_iota(jnp.int32, (size, size), 1)
        return jnp.where(a < b if lower_first else b < a, 1.0, 0.0).astype(jnp.bfloat16)

    lane_before = below_than(LANES, True)
    row_before = below_than(HIGHS, False)
    lane_ids = lax.broadcasted_iota(jnp.int32, (8, LANES), 1)
    bound = devices * per * LANES

    def share(at):
        @pl.loop(1, slots)
        def _(k):
            d = x * group + own_copy * slots + lax.rem(slot + k, slots)
            pltpu.make_async_remote_copy(
                src_ref=res.at[at],
                dst_ref=res.at[at],
                send_sem=res_send_sem,
                recv_sem=res_recv_sem,
                device_id=place(d),
                device_id_type=MESH,
            ).start()

    for i in range(held):
        total = totals[i]
        at = slot * held + i
        own = pl.ds(pl.multiple_of(x * blocks, blocks), blocks)
        own_neg = pl.ds(pl.multiple_of(HIGHS + x * blocks, blocks), blocks)
        positives, negatives = totals[i, own, :], totals[i, own_neg, :]
        count = jnp.maximum(positives + negatives, 1.0)
        report = [positives / count]
        for k in range(3):
            first = 2 * HIGHS + k * blocks
            second = first + 3 * blocks
            value = total[first : first + blocks] + total[second : second + blocks]
            report.append(value / count)
        for k in range(4):
            res[at, k : k + 1, 0:span] = jnp.concatenate(
                [report[k][h : h + 1] for h in range(blocks)], axis=1
            )
        pos, neg = total[:HIGHS], total[HIGHS : 2 * HIGHS]
        lane_below = jnp.zeros((HIGHS, LANES), jnp.float32)
        rows_below = jnp.zeros((HIGHS, LANES), jnp.float32)
        for digit, scale in exact_digits(neg, bound):
            digit = digit.astype(jnp.bfloat16)
            lane_below += scale * jnp.dot(
                digit, lane_before, preferred_element_type=jnp.float32
            )
            rows_below += scale * jnp.dot(
                row_before, digit, preferred_element_type=jnp.float32
            )
        below = lane_below + jnp.sum(rows_below, axis=1, keepdims=True)
        sums = [pos * (below + 0.5 * neg), pos, neg]
        sums = [jnp.sum(a, axis=0, keepdims=True) for a in sums]
        for k in range(3):
            part = jnp.sum(vals[:, :, k, i * per : (i + 1) * per, :], axis=(0, 1))
            sums.append(jnp.sum(part, axis=0, keepdims=True))
        sums += [jnp.zeros((1, LANES), jnp.float32)] * 2
        sums = jnp.sum(jnp.concatenate(sums, axis=0), axis=1, keepdims=True)
        numerator, p_sum, n_sum, s_p, s_loss, s_sq = (sums[k : k + 1] for k in range(6))
        examples = jnp.maximum(p_sum + n_sum, 1.0)
        line = jnp.where(lane_ids == 0, numerator / jnp.maximum(p_sum * n_sum, 1.0), 0.0)
        line = jnp.where(lane_ids == 1, s_loss / examples, line)
        line = jnp.where(lane_ids == 2, s_p / jnp.maximum(p_sum, 1.0), line)
        line = jnp.where(lane_ids == 3, s_sq / examples, line)
        res[at, :, span:] = line[0:4]
        share(at)

    others = res.at[pl.ds(0, intervals - held)]
    if slots > 1:
        pltpu.make_async_copy(others, others, res_recv_sem).wait()
    reports = pltpu.make_async_copy(res.at[:, :, pl.ds(0, span)], stats_ref, out_sem)
    reports.start()
    summary_ref[...] = res[:, 0:1, span:]
    reports.wait()
    if slots > 1:
        pltpu.make_async_copy(others, others, res_send_sem).wait()
    for i in range(slots):
        count = reps - 1 if i == last else reps
        if count:
            sent = got.at[i, pl.ds(0, count)]
            pltpu.make_async_copy(sent, sent, send_sem.at[i]).wait()


def on_device(sizes, *args):
    (
        interact,
        weight_one,
        bias_one,
        weight_two,
        bias_two,
        weight_three,
        bias_three,
        weight_four,
        bias_four,
        weight_out,
        bias_out,
        bucket_index,
        labels,
    ) = args
    intervals, rows, features = interact.shape
    nx, ny, nz = sizes
    devices = nx * ny * nz
    slots = min(ny * nz, intervals)
    pair = PAIR if slots % PAIR == 0 else 1
    held = intervals // slots
    tile = held * rows
    lines = tile // LANES
    blocks = HIGHS // nx
    reps = devices // slots
    weights = (weight_one, weight_two, weight_three, weight_four)
    operands = [
        interact.reshape(slots, tile, features),
        weight_one,
        bias_one.reshape(1, -1),
        weight_two,
        bias_two.reshape(1, -1),
        weight_three,
        bias_three.reshape(1, -1),
        weight_four,
        bias_four.reshape(1, -1),
        weight_out.reshape(1, -1),
        bias_out,
        bucket_index,
        labels,
    ]
    vmem = pl.BlockSpec(memory_space=pltpu.VMEM)
    in_specs = [pl.BlockSpec(memory_space=pltpu.HBM)] * len(operands)
    in_specs[10] = pl.BlockSpec(memory_space=pltpu.SMEM)
    stats, summary = pl.pallas_call(
        functools.partial(report_kernel, sizes, slots),
        in_specs=in_specs,
        out_specs=[pl.BlockSpec(memory_space=pltpu.HBM), vmem],
        out_shape=[
            jax.ShapeDtypeStruct((intervals, 4, blocks * LANES), jnp.float32),
            jax.ShapeDtypeStruct((intervals, 1, LANES), jnp.float32),
        ],
        scratch_shapes=[pltpu.VMEM(a.shape, a.dtype) for k, a in enumerate(operands) if k != 10]
        + [pltpu.VMEM((pair, tile, w.shape[1]), jnp.bfloat16) for w in weights]
        + [
            pltpu.VMEM((slots, 3, lines, LANES), jnp.float32),
            pltpu.VMEM((slots, reps, 3, lines, LANES), jnp.float32),
            pltpu.VMEM((slots, reps, 3, lines, LANES), jnp.float32),
            pltpu.VMEM((held, 2 * HIGHS + 6 * blocks, LANES), jnp.float32),
            pltpu.VMEM((intervals, 4, (blocks + 1) * LANES), jnp.float32),
            pltpu.SemaphoreType.DMA((slots,)),
            pltpu.SemaphoreType.DMA((11,)),
            pltpu.SemaphoreType.DMA((slots,)),
            pltpu.SemaphoreType.DMA((slots,)),
            pltpu.SemaphoreType.DMA,
            pltpu.SemaphoreType.DMA,
            pltpu.SemaphoreType.DMA,
        ],
        compiler_params=pltpu.CompilerParams(
            collective_id=0, has_side_effects=True, vmem_limit_bytes=60 * 2**20
        ),
        name="report",
    )(*operands)
    return stats, summary[:, 0, :4]


def solution(mesh):
    sizes = tuple(mesh.shape[a] for a in AXES)
    in_specs = (
        (P(None, AXES, None),) + (P(),) * 10 + (P(None, AXES), P(None, AXES))
    )
    out_specs = (P(None, None, "gx"), P())
    return jax.shard_map(
        functools.partial(on_device, sizes),
        mesh=mesh,
        in_specs=in_specs,
        out_specs=out_specs,
        check_vma=False,
    )
```

```python
import functools

import jax
import jax.numpy as jnp
from jax import lax
from jax.experimental import pallas as pl
from jax.experimental.pallas import tpu as pltpu
from jax.sharding import PartitionSpec as P

NBUCK = 4096
LANES = 128
PAIR = 2
HIGHS = NBUCK // LANES
MESH = pl.DeviceIdType.MESH
AXES = ("gx", "gy", "gz")


def exact_digits(a, bound):
    digits, scale = [], 1.0
    while True:
        if bound <= 256:
            return digits + [(a, scale)]
        upper = jnp.floor(a * (1.0 / 256.0))
        digits.append((a - 256.0 * upper, scale))
        a, bound, scale = upper, bound // 256, scale * 256.0


def report_kernel(
    sizes,
    slots,
    x_hbm,
    w1_hbm,
    b1_hbm,
    w2_hbm,
    b2_hbm,
    w3_hbm,
    b3_hbm,
    w4_hbm,
    b4_hbm,
    wo_hbm,
    bo_ref,
    bucket_hbm,
    label_hbm,
    stats_ref,
    summary_ref,
    x_ref,
    w1_ref,
    b1_ref,
    w2_ref,
    b2_ref,
    w3_ref,
    b3_ref,
    w4_ref,
    b4_ref,
    wo_ref,
    bucket_ref,
    label_ref,
    hidden_one,
    hidden_two,
    hidden_three,
    hidden_four,
    packed,
    got,
    vals,
    totals,
    res,
    x_sem,
    w_sem,
    send_sem,
    recv_sem,
    res_send_sem,
    res_recv_sem,
    out_sem,
):
    nx, ny, nz = sizes
    group = ny * nz
    devices = nx * group
    x, y, z = (lax.axis_index(a) for a in AXES)
    mine = y * nz + z
    me = x * group + mine
    slot = lax.rem(mine, slots)
    own_copy = mine // slots
    copies = group // slots
    intervals = stats_ref.shape[0]
    held = intervals // slots
    span = stats_ref.shape[2]
    blocks = span // LANES
    tile = x_ref.shape[1]
    lines = tile // LANES
    per = lines // held
    reps = nx * copies
    here = x * copies + own_copy
    pair = PAIR if slots % PAIR == 0 else 1

    def place(d):
        inner = lax.rem(d, group)
        return (d // group, inner // nz, lax.rem(inner, nz))

    def turn(i):
        return lax.rem(slot + 1 + i, slots)

    loads = {}
    pairs = (
        ("w1", w1_hbm, w1_ref),
        ("b1", b1_hbm, b1_ref),
        ("w2", w2_hbm, w2_ref),
        ("b2", b2_hbm, b2_ref),
        ("w3", w3_hbm, w3_ref),
        ("b3", b3_hbm, b3_ref),
        ("w4", w4_hbm, w4_ref),
        ("b4", b4_hbm, b4_ref),
        ("wo", wo_hbm, wo_ref),
        ("bucket", bucket_hbm, bucket_ref),
        ("label", label_hbm, label_ref),
    )

    def x_load(i):
        at = turn(i)
        return pltpu.make_async_copy(x_hbm.at[at], x_ref.at[at], x_sem.at[i])

    x_load(0).start()
    for k, (key, src, dst) in enumerate(pairs):
        loads[key] = pltpu.make_async_copy(src, dst, w_sem.at[k])
        loads[key].start()
        if key == "b1":
            for i in range(1, PAIR if slots % PAIR == 0 else 1):
                x_load(i).start()
    for i in range(PAIR if slots % PAIR == 0 else 1, slots):
        x_load(i).start()

    barrier = pltpu.get_barrier_semaphore()

    @pl.loop(1, devices)
    def _(k):
        d = lax.rem(me + k, devices)
        pl.semaphore_signal(barrier, inc=1, device_id=place(d), device_id_type=MESH)

    def layer(src, w_ref, b_ref, dst):
        for col in range(0, w_ref.shape[1], 256):
            cols = slice(col, col + 256)
            acc = jnp.dot(src[...], w_ref[:, cols], preferred_element_type=jnp.float32)
            dst[:, cols] = jnp.maximum(acc + b_ref[:, cols], 0.0).astype(jnp.bfloat16)

    def scores(order, first):
        def need(*keys):
            if first:
                for key in keys:
                    loads[key].wait()

        where = [turn(i) for i in order]
        for i in order:
            x_load(i).wait()
        need("w1", "b1")
        for p, c in enumerate(where):
            layer(x_ref.at[c], w1_ref, b1_ref, hidden_one.at[p])
        need("w2", "b2")
        for p, c in enumerate(where):
            layer(hidden_one.at[p], w2_ref, b2_ref, hidden_two.at[p])
        need("w3", "b3")
        for p, c in enumerate(where):
            layer(hidden_two.at[p], w3_ref, b3_ref, hidden_three.at[p])
        need("w4", "b4")
        for p, c in enumerate(where):
            layer(hidden_three.at[p], w4_ref, b4_ref, hidden_four.at[p])
        need("wo")
        wide = jnp.broadcast_to(wo_ref[...].astype(jnp.float32), (16, wo_ref.shape[1]))
        for p, c in enumerate(where):
            logits = lax.dot_general(
                wide.astype(jnp.bfloat16),
                hidden_four[p],
                (((1,), (1,)), ((), ())),
                preferred_element_type=jnp.float32,
            )[0:1] + bo_ref[0]
            for row in range(lines):
                packed[c, 0, row : row + 1, :] = logits[:, row * LANES : (row + 1) * LANES]

    def send(i):
        c = turn(i)
        for k in range(reps):
            rep = lax.rem(here + k, reps)
            inner = lax.rem(rep, copies) * slots + c
            remote = pltpu.make_async_remote_copy(
                src_ref=packed.at[c],
                dst_ref=got.at[i, here],
                send_sem=send_sem.at[i],
                recv_sem=recv_sem.at[i],
                device_id=(rep // copies, inner // nz, lax.rem(inner, nz)),
                device_id_type=MESH,
            )
            if k == 0:
                pl.when(c != slot)(remote.start)
            else:
                remote.start()

    def arrived(i):
        pltpu.make_async_copy(got.at[i], got.at[i], recv_sem.at[i]).wait()

    turns = next(b for b in (max(8 // reps, 1), 1) if slots % b == 0)
    sources = [(t, n) for t in range(turns) for n in range(reps)]
    width = len(sources) * per * LANES
    low_ids = lax.broadcasted_iota(jnp.int32, (LANES, LANES), 1)
    high_ids = lax.broadcasted_iota(jnp.int32, (HIGHS, width), 0)
    block_ids = lax.broadcasted_iota(jnp.int32, (blocks, width), 0) + x * blocks

    def measure_all():
        logit = got[:, :, 0]
        label = got[:, :, 2]
        small = jnp.exp(-jnp.abs(logit))
        predicted = jnp.where(logit >= 0.0, 1.0, small) / (1.0 + small)
        vals[:, :, 0] = predicted
        vals[:, :, 1] = jnp.maximum(logit, 0.0) + jnp.log1p(small) - label * logit
        vals[:, :, 2] = (predicted - label) ** 2

    def add(step, carry):
        first = step * turns
        ids = jnp.concatenate([got[first + t, n, 1] for t, n in sources], axis=0)
        down = jnp.transpose(ids).astype(jnp.int32) & (LANES - 1)
        out = []
        for e in range(held):

            def line(ref, k):
                return jnp.concatenate(
                    [
                        ref[first + t, n, k, row : row + 1, :]
                        for t, n in sources
                        for row in range(e * per, (e + 1) * per)
                    ],
                    axis=1,
                )

            columns = [
                q * lines + row
                for q in range(len(sources))
                for row in range(e * per, (e + 1) * per)
            ]
            one_hot = jnp.concatenate(
                [jnp.where(low_ids == down[:, c : c + 1], 1.0, 0.0) for c in columns], axis=0
            ).astype(jnp.bfloat16)
            bucket = line(got, 1).astype(jnp.int32)
            observed = line(got, 2)
            high = lax.shift_right_logical(bucket, LANES.bit_length() - 1)
            at_high = high_ids == high
            at_block = block_ids == high
            parts = [
                jnp.where(at_high, observed, 0.0),
                jnp.where(at_high, 1.0 - observed, 0.0),
            ]
            lower = []
            for k in range(3):
                value = line(vals, k)
                upper = value.astype(jnp.bfloat16).astype(jnp.float32)
                parts.append(jnp.where(at_block, upper, 0.0))
                lower.append(jnp.where(at_block, value - upper, 0.0))
            left = jnp.concatenate(parts + lower, axis=0).astype(jnp.bfloat16)
            out.append(
                carry[e] + jnp.dot(left, one_hot, preferred_element_type=jnp.float32)
            )
        return tuple(out)

    scores(range(pair), True)

    loads["bucket"].wait()
    loads["label"].wait()
    for i in range(intervals):
        for j in range(per):
            c, row = divmod(i * per + j, lines)
            cols = slice(j * LANES, (j + 1) * LANES)
            packed[c, 1, row : row + 1, :] = bucket_ref[i : i + 1, cols].astype(jnp.float32)
            packed[c, 2, row : row + 1, :] = label_ref[i : i + 1, cols].astype(jnp.float32)

    pl.semaphore_wait(barrier, devices - 1)
    for i in range(pair):
        send(i)

    @pl.loop(1, slots // pair)
    def _(step):
        order = [step * pair + p for p in range(pair)]
        scores(order, False)
        for i in order:
            send(i)

    last = slots - 1
    pltpu.make_async_copy(packed.at[slot], got.at[last, here], recv_sem.at[last]).start()
    for i in range(slots):
        arrived(i)
    measure_all()
    zero = jnp.zeros(totals.shape[1:], jnp.float32)
    sums = lax.fori_loop(0, slots // turns, add, (zero,) * held)
    for e in range(held):
        totals[e] = sums[e]

    def below_than(size, lower_first):
        a = lax.broadcasted_iota(jnp.int32, (size, size), 0)
        b = lax.broadcasted_iota(jnp.int32, (size, size), 1)
        return jnp.where(a < b if lower_first else b < a, 1.0, 0.0).astype(jnp.bfloat16)

    lane_before = below_than(LANES, True)
    row_before = below_than(HIGHS, False)
    lane_ids = lax.broadcasted_iota(jnp.int32, (8, LANES), 1)
    bound = devices * per * LANES

    def share(at):
        @pl.loop(1, slots)
        def _(k):
            d = x * group + own_copy * slots + lax.rem(slot + k, slots)
            pltpu.make_async_remote_copy(
                src_ref=res.at[at],
                dst_ref=res.at[at],
                send_sem=res_send_sem,
                recv_sem=res_recv_sem,
                device_id=place(d),
                device_id_type=MESH,
            ).start()

    for i in range(held):
        total = totals[i]
        at = slot * held + i
        own = pl.ds(pl.multiple_of(x * blocks, blocks), blocks)
        own_neg = pl.ds(pl.multiple_of(HIGHS + x * blocks, blocks), blocks)
        positives, negatives = totals[i, own, :], totals[i, own_neg, :]
        count = jnp.maximum(positives + negatives, 1.0)
        report = [positives / count]
        for k in range(3):
            first = 2 * HIGHS + k * blocks
            second = first + 3 * blocks
            value = total[first : first + blocks] + total[second : second + blocks]
            report.append(value / count)
        for k in range(4):
            res[at, k : k + 1, 0:span] = jnp.concatenate(
                [report[k][h : h + 1] for h in range(blocks)], axis=1
            )
        pos, neg = total[:HIGHS], total[HIGHS : 2 * HIGHS]
        lane_below = jnp.zeros((HIGHS, LANES), jnp.float32)
        rows_below = jnp.zeros((HIGHS, LANES), jnp.float32)
        for digit, scale in exact_digits(neg, bound):
            digit = digit.astype(jnp.bfloat16)
            lane_below += scale * jnp.dot(
                digit, lane_before, preferred_element_type=jnp.float32
            )
            rows_below += scale * jnp.dot(
                row_before, digit, preferred_element_type=jnp.float32
            )
        below = lane_below + jnp.sum(rows_below, axis=1, keepdims=True)
        sums = [pos * (below + 0.5 * neg), pos, neg]
        sums = [jnp.sum(a, axis=0, keepdims=True) for a in sums]
        for k in range(3):
            part = jnp.sum(vals[:, :, k, i * per : (i + 1) * per, :], axis=(0, 1))
            sums.append(jnp.sum(part, axis=0, keepdims=True))
        sums += [jnp.zeros((1, LANES), jnp.float32)] * 2
        sums = jnp.sum(jnp.concatenate(sums, axis=0), axis=1, keepdims=True)
        numerator, p_sum, n_sum, s_p, s_loss, s_sq = (sums[k : k + 1] for k in range(6))
        examples = jnp.maximum(p_sum + n_sum, 1.0)
        line = jnp.where(lane_ids == 0, numerator / jnp.maximum(p_sum * n_sum, 1.0), 0.0)
        line = jnp.where(lane_ids == 1, s_loss / examples, line)
        line = jnp.where(lane_ids == 2, s_p / jnp.maximum(p_sum, 1.0), line)
        line = jnp.where(lane_ids == 3, s_sq / examples, line)
        res[at, :, span:] = line[0:4]
        share(at)

    others = res.at[pl.ds(0, intervals - held)]
    if slots > 1:
        pltpu.make_async_copy(others, others, res_recv_sem).wait()
    reports = pltpu.make_async_copy(res.at[:, :, pl.ds(0, span)], stats_ref, out_sem)
    reports.start()
    pick = jnp.where(
        lax.broadcasted_iota(jnp.int32, (8, LANES), 0)
        == lax.broadcasted_iota(jnp.int32, (8, LANES), 1),
        1.0,
        0.0,
    )
    summary_ref[...] = lax.dot_general(
        pick,
        res[:, 0, span:],
        (((1,), (1,)), ((), ())),
        preferred_element_type=jnp.float32,
        precision=lax.Precision.HIGHEST,
    )[:4]
    reports.wait()
    if slots > 1:
        pltpu.make_async_copy(others, others, res_send_sem).wait()
    for i in range(slots):
        count = reps - 1 if i == last else reps
        if count:
            sent = got.at[i, pl.ds(0, count)]
            pltpu.make_async_copy(sent, sent, send_sem.at[i]).wait()


def on_device(sizes, *args):
    (
        interact,
        weight_one,
        bias_one,
        weight_two,
        bias_two,
        weight_three,
        bias_three,
        weight_four,
        bias_four,
        weight_out,
        bias_out,
        bucket_index,
        labels,
    ) = args
    intervals, rows, features = interact.shape
    nx, ny, nz = sizes
    devices = nx * ny * nz
    slots = min(ny * nz, intervals)
    pair = PAIR if slots % PAIR == 0 else 1
    held = intervals // slots
    tile = held * rows
    lines = tile // LANES
    blocks = HIGHS // nx
    reps = devices // slots
    weights = (weight_one, weight_two, weight_three, weight_four)
    operands = [
        interact.reshape(slots, tile, features),
        weight_one,
        bias_one.reshape(1, -1),
        weight_two,
        bias_two.reshape(1, -1),
        weight_three,
        bias_three.reshape(1, -1),
        weight_four,
        bias_four.reshape(1, -1),
        weight_out.reshape(1, -1),
        bias_out,
        bucket_index,
        labels,
    ]
    vmem = pl.BlockSpec(memory_space=pltpu.VMEM)
    in_specs = [pl.BlockSpec(memory_space=pltpu.HBM)] * len(operands)
    in_specs[10] = pl.BlockSpec(memory_space=pltpu.SMEM)
    stats, summary = pl.pallas_call(
        functools.partial(report_kernel, sizes, slots),
        in_specs=in_specs,
        out_specs=[pl.BlockSpec(memory_space=pltpu.HBM), vmem],
        out_shape=[
            jax.ShapeDtypeStruct((intervals, 4, blocks * LANES), jnp.float32),
            jax.ShapeDtypeStruct((4, intervals), jnp.float32),
        ],
        scratch_shapes=[pltpu.VMEM(a.shape, a.dtype) for k, a in enumerate(operands) if k != 10]
        + [pltpu.VMEM((pair, tile, w.shape[1]), jnp.bfloat16) for w in weights]
        + [
            pltpu.VMEM((slots, 3, lines, LANES), jnp.float32),
            pltpu.VMEM((slots, reps, 3, lines, LANES), jnp.float32),
            pltpu.VMEM((slots, reps, 3, lines, LANES), jnp.float32),
            pltpu.VMEM((held, 2 * HIGHS + 6 * blocks, LANES), jnp.float32),
            pltpu.VMEM((intervals, 4, (blocks + 1) * LANES), jnp.float32),
            pltpu.SemaphoreType.DMA((slots,)),
            pltpu.SemaphoreType.DMA((11,)),
            pltpu.SemaphoreType.DMA((slots,)),
            pltpu.SemaphoreType.DMA((slots,)),
            pltpu.SemaphoreType.DMA,
            pltpu.SemaphoreType.DMA,
            pltpu.SemaphoreType.DMA,
        ],
        compiler_params=pltpu.CompilerParams(
            collective_id=0, has_side_effects=True, vmem_limit_bytes=60 * 2**20
        ),
        name="report",
    )(*operands)
    return stats, summary.T


def solution(mesh):
    sizes = tuple(mesh.shape[a] for a in AXES)
    in_specs = (
        (P(None, AXES, None),) + (P(),) * 10 + (P(None, AXES), P(None, AXES))
    )
    out_specs = (P(None, None, "gx"), P())
    return jax.shard_map(
        functools.partial(on_device, sizes),
        mesh=mesh,
        in_specs=in_specs,
        out_specs=out_specs,
        check_vma=False,
    )
```

```python
import functools

import jax
import jax.numpy as jnp
from jax import lax
from jax.experimental import pallas as pl
from jax.experimental.pallas import tpu as pltpu
from jax.sharding import PartitionSpec as P

NBUCK = 4096
LANES = 128
PAIR = 2
HIGHS = NBUCK // LANES
MESH = pl.DeviceIdType.MESH
AXES = ("gx", "gy", "gz")


def exact_digits(a, bound):
    digits, scale = [], 1.0
    while True:
        if bound <= 256:
            return digits + [(a, scale)]
        upper = jnp.floor(a * (1.0 / 256.0))
        digits.append((a - 256.0 * upper, scale))
        a, bound, scale = upper, bound // 256, scale * 256.0


def report_kernel(
    sizes,
    slots,
    x_hbm,
    w1_hbm,
    b1_hbm,
    w2_hbm,
    b2_hbm,
    w3_hbm,
    b3_hbm,
    w4_hbm,
    b4_hbm,
    wo_hbm,
    bo_ref,
    bucket_hbm,
    label_hbm,
    stats_ref,
    summary_ref,
    x_ref,
    w1_ref,
    b1_ref,
    w2_ref,
    b2_ref,
    w3_ref,
    b3_ref,
    w4_ref,
    b4_ref,
    wo_ref,
    bucket_ref,
    label_ref,
    hidden_one,
    hidden_two,
    hidden_three,
    hidden_four,
    packed,
    got,
    vals,
    totals,
    res,
    x_sem,
    w_sem,
    send_sem,
    recv_sem,
    res_send_sem,
    res_recv_sem,
    out_sem,
):
    nx, ny, nz = sizes
    group = ny * nz
    devices = nx * group
    x, y, z = (lax.axis_index(a) for a in AXES)
    mine = y * nz + z
    me = x * group + mine
    slot = lax.rem(mine, slots)
    own_copy = mine // slots
    copies = group // slots
    intervals = stats_ref.shape[0]
    held = intervals // slots
    span = stats_ref.shape[2]
    blocks = span // LANES
    tile = x_ref.shape[1]
    lines = tile // LANES
    per = lines // held
    reps = nx * copies
    here = x * copies + own_copy
    pair = PAIR if slots % PAIR == 0 else 1

    def place(d):
        inner = lax.rem(d, group)
        return (d // group, inner // nz, lax.rem(inner, nz))

    def turn(i):
        return lax.rem(slot + 1 + i, slots)

    loads = {}
    pairs = (
        ("w1", w1_hbm, w1_ref),
        ("b1", b1_hbm, b1_ref),
        ("w2", w2_hbm, w2_ref),
        ("b2", b2_hbm, b2_ref),
        ("w3", w3_hbm, w3_ref),
        ("b3", b3_hbm, b3_ref),
        ("w4", w4_hbm, w4_ref),
        ("b4", b4_hbm, b4_ref),
        ("wo", wo_hbm, wo_ref),
        ("bucket", bucket_hbm, bucket_ref),
        ("label", label_hbm, label_ref),
    )

    def x_load(i):
        at = turn(i)
        return pltpu.make_async_copy(x_hbm.at[at], x_ref.at[at], x_sem.at[i])

    x_load(0).start()
    for k, (key, src, dst) in enumerate(pairs):
        loads[key] = pltpu.make_async_copy(src, dst, w_sem.at[k])
        loads[key].start()
        if key == "b1":
            for i in range(1, PAIR if slots % PAIR == 0 else 1):
                x_load(i).start()
    for i in range(PAIR if slots % PAIR == 0 else 1, slots):
        x_load(i).start()

    barrier = pltpu.get_barrier_semaphore()

    @pl.loop(1, devices)
    def _(k):
        d = lax.rem(me + k, devices)
        pl.semaphore_signal(barrier, inc=1, device_id=place(d), device_id_type=MESH)

    def layer(src, w_ref, b_ref, dst):
        for col in range(0, w_ref.shape[1], 256):
            cols = slice(col, col + 256)
            acc = jnp.dot(src[...], w_ref[:, cols], preferred_element_type=jnp.float32)
            dst[:, cols] = jnp.maximum(acc + b_ref[:, cols], 0.0).astype(jnp.bfloat16)

    def scores(order, first):
        def need(*keys):
            if first:
                for key in keys:
                    loads[key].wait()

        where = [turn(i) for i in order]
        for i in order:
            x_load(i).wait()
        need("w1", "b1")
        for p, c in enumerate(where):
            layer(x_ref.at[c], w1_ref, b1_ref, hidden_one.at[p])
        need("w2", "b2")
        for p, c in enumerate(where):
            layer(hidden_one.at[p], w2_ref, b2_ref, hidden_two.at[p])
        need("w3", "b3")
        for p, c in enumerate(where):
            layer(hidden_two.at[p], w3_ref, b3_ref, hidden_three.at[p])
        need("w4", "b4")
        for p, c in enumerate(where):
            layer(hidden_three.at[p], w4_ref, b4_ref, hidden_four.at[p])
        need("wo")
        wide = jnp.broadcast_to(wo_ref[...].astype(jnp.float32), (16, wo_ref.shape[1]))
        for p, c in enumerate(where):
            logits = lax.dot_general(
                wide.astype(jnp.bfloat16),
                hidden_four[p],
                (((1,), (1,)), ((), ())),
                preferred_element_type=jnp.float32,
            )[0:1] + bo_ref[0]
            for row in range(lines):
                packed[c, 0, row : row + 1, :] = logits[:, row * LANES : (row + 1) * LANES]

    def send(i):
        c = turn(i)
        for k in range(reps):
            rep = lax.rem(here + k, reps)
            inner = lax.rem(rep, copies) * slots + c
            remote = pltpu.make_async_remote_copy(
                src_ref=packed.at[c],
                dst_ref=got.at[i, here],
                send_sem=send_sem.at[i],
                recv_sem=recv_sem.at[i],
                device_id=(rep // copies, inner // nz, lax.rem(inner, nz)),
                device_id_type=MESH,
            )
            if k == 0:
                pl.when(c != slot)(remote.start)
            else:
                remote.start()

    def arrived(i):
        pltpu.make_async_copy(got.at[i], got.at[i], recv_sem.at[i]).wait()

    turns = next(b for b in (max(8 // reps, 1), 1) if slots % b == 0)
    sources = [(t, n) for t in range(turns) for n in range(reps)]
    width = len(sources) * per * LANES
    half = jnp.bfloat16
    tall = max(blocks, 16)
    step_ids = lax.broadcasted_iota(jnp.int32, (16, width), 0)

    def rows_of(row):
        return jnp.broadcast_to(row, (16, width)).astype(half)

    def spread(ids, first, count, values):
        masks = [
            (step_ids + (first + r)).astype(jnp.float32).astype(half) == ids
            for r in range(0, count, 16)
        ]
        zero = jnp.zeros((16, width), half)
        return [jnp.where(mask, value, zero) for value in values for mask in masks]

    def measure_all():
        logit = got[:, :, 0]
        label = got[:, :, 2]
        small = jnp.exp(-jnp.abs(logit))
        predicted = jnp.where(logit >= 0.0, 1.0, small) / (1.0 + small)
        vals[:, :, 0] = predicted
        vals[:, :, 1] = jnp.maximum(logit, 0.0) + jnp.log1p(small) - label * logit
        vals[:, :, 2] = (predicted - label) ** 2

    def add(step, carry):
        first = step * turns
        out = []
        for e in range(held):

            def line(ref, k):
                return jnp.concatenate(
                    [
                        ref[first + t, n, k, row : row + 1, :]
                        for t, n in sources
                        for row in range(e * per, (e + 1) * per)
                    ],
                    axis=1,
                )

            bucket = line(got, 1).astype(jnp.int32)
            low = rows_of((bucket & (LANES - 1)).astype(jnp.float32))
            high = rows_of(
                lax.shift_right_logical(bucket, LANES.bit_length() - 1).astype(jnp.float32)
            )
            observed = line(got, 2)
            labels = [rows_of(observed), rows_of(1.0 - observed)]
            values = [rows_of(line(vals, k)) for k in range(3)]
            one_hot = jnp.concatenate(
                spread(low, 0, LANES, [jnp.ones((16, width), half)]), axis=0
            )
            left = jnp.concatenate(
                spread(high, 0, HIGHS, labels) + spread(high, x * blocks, tall, values), axis=0
            )
            out.append(
                carry[e]
                + lax.dot_general(
                    left, one_hot, (((1,), (1,)), ((), ())), preferred_element_type=jnp.float32
                )
            )
        return tuple(out)

    scores(range(pair), True)

    loads["bucket"].wait()
    loads["label"].wait()
    for i in range(intervals):
        for j in range(per):
            c, row = divmod(i * per + j, lines)
            cols = slice(j * LANES, (j + 1) * LANES)
            packed[c, 1, row : row + 1, :] = bucket_ref[i : i + 1, cols].astype(jnp.float32)
            packed[c, 2, row : row + 1, :] = label_ref[i : i + 1, cols].astype(jnp.float32)

    pl.semaphore_wait(barrier, devices - 1)
    for i in range(pair):
        send(i)

    @pl.loop(1, slots // pair)
    def _(step):
        order = [step * pair + p for p in range(pair)]
        scores(order, False)
        for i in order:
            send(i)

    last = slots - 1
    pltpu.make_async_copy(packed.at[slot], got.at[last, here], recv_sem.at[last]).start()
    for i in range(slots):
        arrived(i)
    measure_all()
    zero = jnp.zeros(totals.shape[1:], jnp.float32)
    sums = lax.fori_loop(0, slots // turns, add, (zero,) * held)
    for e in range(held):
        totals[e] = sums[e]

    def below_than(size, lower_first):
        a = lax.broadcasted_iota(jnp.int32, (size, size), 0)
        b = lax.broadcasted_iota(jnp.int32, (size, size), 1)
        return jnp.where(a < b if lower_first else b < a, 1.0, 0.0).astype(jnp.bfloat16)

    lane_before = below_than(LANES, True)
    row_before = below_than(HIGHS, False)
    lane_ids = lax.broadcasted_iota(jnp.int32, (8, LANES), 1)
    bound = devices * per * LANES

    for i in range(held):
        total = totals[i]
        at = slot * held + i
        own = pl.ds(pl.multiple_of(x * blocks, blocks), blocks)
        own_neg = pl.ds(pl.multiple_of(HIGHS + x * blocks, blocks), blocks)
        positives, negatives = totals[i, own, :], totals[i, own_neg, :]
        count = jnp.maximum(positives + negatives, 1.0)
        report = [positives / count]
        for k in range(3):
            first = 2 * HIGHS + k * tall
            report.append(total[first : first + blocks] / count)
        for k in range(4):
            res[at, k : k + 1, 0:span] = jnp.concatenate(
                [report[k][h : h + 1] for h in range(blocks)], axis=1
            )
        pos, neg = total[:HIGHS], total[HIGHS : 2 * HIGHS]
        lane_below = jnp.zeros((HIGHS, LANES), jnp.float32)
        rows_below = jnp.zeros((HIGHS, LANES), jnp.float32)
        for digit, scale in exact_digits(neg, bound):
            digit = digit.astype(jnp.bfloat16)
            lane_below += scale * jnp.dot(
                digit, lane_before, preferred_element_type=jnp.float32
            )
            rows_below += scale * jnp.dot(
                row_before, digit, preferred_element_type=jnp.float32
            )
        below = lane_below + jnp.sum(rows_below, axis=1, keepdims=True)
        sums = [pos * (below + 0.5 * neg), pos, neg]
        sums = [jnp.sum(a, axis=0, keepdims=True) for a in sums]
        for k in range(3):
            part = jnp.sum(vals[:, :, k, i * per : (i + 1) * per, :], axis=(0, 1))
            sums.append(jnp.sum(part, axis=0, keepdims=True))
        sums += [jnp.zeros((1, LANES), jnp.float32)] * 2
        sums = jnp.sum(jnp.concatenate(sums, axis=0), axis=1, keepdims=True)
        numerator, p_sum, n_sum, s_p, s_loss, s_sq = (sums[k : k + 1] for k in range(6))
        examples = jnp.maximum(p_sum + n_sum, 1.0)
        line = jnp.where(lane_ids == 0, numerator / jnp.maximum(p_sum * n_sum, 1.0), 0.0)
        line = jnp.where(lane_ids == 1, s_loss / examples, line)
        line = jnp.where(lane_ids == 2, s_p / jnp.maximum(p_sum, 1.0), line)
        line = jnp.where(lane_ids == 3, s_sq / examples, line)
        res[at, :, span:] = line[0:4]

    own = pl.ds(slot * held, held)

    @pl.loop(1, slots)
    def _(k):
        d = x * group + own_copy * slots + lax.rem(slot + k, slots)
        pltpu.make_async_remote_copy(
            src_ref=res.at[own],
            dst_ref=res.at[own],
            send_sem=res_send_sem,
            recv_sem=res_recv_sem,
            device_id=place(d),
            device_id_type=MESH,
        ).start()

    others = res.at[pl.ds(0, intervals - held)]
    if slots > 1:
        pltpu.make_async_copy(others, others, res_recv_sem).wait()
    reports = pltpu.make_async_copy(res.at[:, :, pl.ds(0, span)], stats_ref, out_sem)
    reports.start()
    pick = jnp.where(
        lax.broadcasted_iota(jnp.int32, (8, LANES), 0)
        == lax.broadcasted_iota(jnp.int32, (8, LANES), 1),
        1.0,
        0.0,
    )
    summary_ref[...] = lax.dot_general(
        pick,
        res[:, 0, span:],
        (((1,), (1,)), ((), ())),
        preferred_element_type=jnp.float32,
        precision=lax.Precision.HIGHEST,
    )[:4]
    reports.wait()
    if slots > 1:
        pltpu.make_async_copy(others, others, res_send_sem).wait()
    for i in range(slots):
        count = reps - 1 if i == last else reps
        if count:
            sent = got.at[i, pl.ds(0, count)]
            pltpu.make_async_copy(sent, sent, send_sem.at[i]).wait()


def finish_kernel(stats_in, summary_in, stats_ref, summary_ref, sems):
    copies = [
        pltpu.make_async_copy(stats_in, stats_ref, sems.at[0]),
        pltpu.make_async_copy(summary_in, summary_ref, sems.at[1]),
    ]
    for copy in copies:
        copy.start()
    for copy in copies:
        copy.wait()


def on_device(sizes, *args):
    (
        interact,
        weight_one,
        bias_one,
        weight_two,
        bias_two,
        weight_three,
        bias_three,
        weight_four,
        bias_four,
        weight_out,
        bias_out,
        bucket_index,
        labels,
    ) = args
    intervals, rows, features = interact.shape
    nx, ny, nz = sizes
    devices = nx * ny * nz
    slots = min(ny * nz, intervals)
    pair = PAIR if slots % PAIR == 0 else 1
    held = intervals // slots
    tile = held * rows
    lines = tile // LANES
    blocks = HIGHS // nx
    reps = devices // slots
    weights = (weight_one, weight_two, weight_three, weight_four)
    operands = [
        interact.reshape(slots, tile, features),
        weight_one,
        bias_one.reshape(1, -1),
        weight_two,
        bias_two.reshape(1, -1),
        weight_three,
        bias_three.reshape(1, -1),
        weight_four,
        bias_four.reshape(1, -1),
        weight_out.reshape(1, -1),
        bias_out,
        bucket_index,
        labels,
    ]
    vmem = pl.BlockSpec(memory_space=pltpu.VMEM)
    in_specs = [pl.BlockSpec(memory_space=pltpu.HBM)] * len(operands)
    in_specs[10] = pl.BlockSpec(memory_space=pltpu.SMEM)
    stats, summary = pl.pallas_call(
        functools.partial(report_kernel, sizes, slots),
        in_specs=in_specs,
        out_specs=[pl.BlockSpec(memory_space=pltpu.HBM), vmem],
        out_shape=[
            jax.ShapeDtypeStruct((intervals, 4, blocks * LANES), jnp.float32),
            jax.ShapeDtypeStruct((4, intervals), jnp.float32),
        ],
        scratch_shapes=[pltpu.VMEM(a.shape, a.dtype) for k, a in enumerate(operands) if k != 10]
        + [pltpu.VMEM((pair, tile, w.shape[1]), jnp.bfloat16) for w in weights]
        + [
            pltpu.VMEM((slots, 3, lines, LANES), jnp.float32),
            pltpu.VMEM((slots, reps, 3, lines, LANES), jnp.float32),
            pltpu.VMEM((slots, reps, 3, lines, LANES), jnp.float32),
            pltpu.VMEM((held, 2 * HIGHS + 3 * max(blocks, 16), LANES), jnp.float32),
            pltpu.VMEM((intervals, 4, (blocks + 1) * LANES), jnp.float32),
            pltpu.SemaphoreType.DMA((slots,)),
            pltpu.SemaphoreType.DMA((11,)),
            pltpu.SemaphoreType.DMA((slots,)),
            pltpu.SemaphoreType.DMA((slots,)),
            pltpu.SemaphoreType.DMA,
            pltpu.SemaphoreType.DMA,
            pltpu.SemaphoreType.DMA,
        ],
        compiler_params=pltpu.CompilerParams(
            collective_id=0, has_side_effects=True, vmem_limit_bytes=60 * 2**20
        ),
        name="report",
    )(*operands)
    hbm = pl.BlockSpec(memory_space=pltpu.HBM)
    stats, summary = pl.pallas_call(
        finish_kernel,
        in_specs=[hbm, hbm],
        out_specs=[hbm, hbm],
        out_shape=[jax.ShapeDtypeStruct(a.shape, a.dtype) for a in (stats, summary)],
        scratch_shapes=[pltpu.SemaphoreType.DMA((2,))],
        compiler_params=pltpu.CompilerParams(vmem_limit_bytes=60 * 2**20),
        name="finish",
    )(stats, summary)
    return stats, summary.T


def solution(mesh):
    sizes = tuple(mesh.shape[a] for a in AXES)
    in_specs = (
        (P(None, AXES, None),) + (P(),) * 10 + (P(None, AXES), P(None, AXES))
    )
    out_specs = (P(None, None, "gx"), P())
    return jax.shard_map(
        functools.partial(on_device, sizes),
        mesh=mesh,
        in_specs=in_specs,
        out_specs=out_specs,
        check_vma=False,
    )
```

```python
import functools

import jax
import jax.numpy as jnp
from jax import lax
from jax.experimental import pallas as pl
from jax.experimental.pallas import tpu as pltpu
from jax.sharding import PartitionSpec as P

NBUCK = 4096
LANES = 128
PAIR = 2
HIGHS = NBUCK // LANES
MESH = pl.DeviceIdType.MESH
AXES = ("gx", "gy", "gz")


def exact_digits(a, bound):
    digits, scale = [], 1.0
    while True:
        if bound <= 256:
            return digits + [(a, scale)]
        upper = jnp.floor(a * (1.0 / 256.0))
        digits.append((a - 256.0 * upper, scale))
        a, bound, scale = upper, bound // 256, scale * 256.0


def report_kernel(
    sizes,
    slots,
    x_hbm,
    w1_hbm,
    b1_hbm,
    w2_hbm,
    b2_hbm,
    w3_hbm,
    b3_hbm,
    w4_hbm,
    b4_hbm,
    wo_hbm,
    bo_ref,
    bucket_hbm,
    label_hbm,
    stats_ref,
    summary_ref,
    x_ref,
    w1_ref,
    b1_ref,
    w2_ref,
    b2_ref,
    w3_ref,
    b3_ref,
    w4_ref,
    b4_ref,
    wo_ref,
    bucket_ref,
    label_ref,
    hidden_one,
    hidden_two,
    hidden_three,
    hidden_four,
    packed,
    got,
    vals,
    totals,
    res,
    x_sem,
    w_sem,
    send_sem,
    recv_sem,
    res_send_sem,
    res_recv_sem,
    out_sem,
):
    nx, ny, nz = sizes
    group = ny * nz
    devices = nx * group
    x, y, z = (lax.axis_index(a) for a in AXES)
    mine = y * nz + z
    me = x * group + mine
    slot = lax.rem(mine, slots)
    own_copy = mine // slots
    copies = group // slots
    intervals = stats_ref.shape[0]
    held = intervals // slots
    span = stats_ref.shape[2]
    blocks = span // LANES
    tile = x_ref.shape[1]
    lines = tile // LANES
    per = lines // held
    reps = nx * copies
    here = x * copies + own_copy
    pair = PAIR if slots % PAIR == 0 else 1

    def place(d):
        inner = lax.rem(d, group)
        return (d // group, inner // nz, lax.rem(inner, nz))

    def turn(i):
        return lax.rem(slot + 1 + i, slots)

    loads = {}
    pairs = (
        ("w1", w1_hbm, w1_ref),
        ("b1", b1_hbm, b1_ref),
        ("w2", w2_hbm, w2_ref),
        ("b2", b2_hbm, b2_ref),
        ("w3", w3_hbm, w3_ref),
        ("b3", b3_hbm, b3_ref),
        ("w4", w4_hbm, w4_ref),
        ("b4", b4_hbm, b4_ref),
        ("wo", wo_hbm, wo_ref),
        ("bucket", bucket_hbm, bucket_ref),
        ("label", label_hbm, label_ref),
    )

    def x_load(i):
        at = turn(i)
        return pltpu.make_async_copy(x_hbm.at[at], x_ref.at[at], x_sem.at[i])

    x_load(0).start()
    for k, (key, src, dst) in enumerate(pairs):
        loads[key] = pltpu.make_async_copy(src, dst, w_sem.at[k])
        loads[key].start()
        if key == "b1":
            for i in range(1, PAIR if slots % PAIR == 0 else 1):
                x_load(i).start()
    for i in range(PAIR if slots % PAIR == 0 else 1, slots):
        x_load(i).start()

    barrier = pltpu.get_barrier_semaphore()

    @pl.loop(1, devices)
    def _(k):
        d = lax.rem(me + k, devices)
        pl.semaphore_signal(barrier, inc=1, device_id=place(d), device_id_type=MESH)

    def layer(src, w_ref, b_ref, dst):
        for col in range(0, w_ref.shape[1], 256):
            cols = slice(col, col + 256)
            acc = jnp.dot(src[...], w_ref[:, cols], preferred_element_type=jnp.float32)
            dst[:, cols] = jnp.maximum(acc + b_ref[:, cols], 0.0).astype(jnp.bfloat16)

    def scores(order, first):
        def need(*keys):
            if first:
                for key in keys:
                    loads[key].wait()

        where = [turn(i) for i in order]
        for i in order:
            x_load(i).wait()
        need("w1", "b1")
        for p, c in enumerate(where):
            layer(x_ref.at[c], w1_ref, b1_ref, hidden_one.at[p])
        need("w2", "b2")
        for p, c in enumerate(where):
            layer(hidden_one.at[p], w2_ref, b2_ref, hidden_two.at[p])
        need("w3", "b3")
        for p, c in enumerate(where):
            layer(hidden_two.at[p], w3_ref, b3_ref, hidden_three.at[p])
        need("w4", "b4")
        for p, c in enumerate(where):
            layer(hidden_three.at[p], w4_ref, b4_ref, hidden_four.at[p])
        need("wo")
        wide = jnp.broadcast_to(wo_ref[...].astype(jnp.float32), (16, wo_ref.shape[1]))
        for p, c in enumerate(where):
            logits = lax.dot_general(
                wide.astype(jnp.bfloat16),
                hidden_four[p],
                (((1,), (1,)), ((), ())),
                preferred_element_type=jnp.float32,
            )[0:1] + bo_ref[0]
            for row in range(lines):
                packed[c, 0, row : row + 1, :] = logits[:, row * LANES : (row + 1) * LANES]

    def send(i):
        c = turn(i)
        for k in range(reps):
            rep = lax.rem(here + k, reps)
            inner = lax.rem(rep, copies) * slots + c
            remote = pltpu.make_async_remote_copy(
                src_ref=packed.at[c],
                dst_ref=got.at[i, here],
                send_sem=send_sem.at[i],
                recv_sem=recv_sem.at[i],
                device_id=(rep // copies, inner // nz, lax.rem(inner, nz)),
                device_id_type=MESH,
            )
            if k == 0:
                pl.when(c != slot)(remote.start)
            else:
                remote.start()

    def arrived(i):
        pltpu.make_async_copy(got.at[i], got.at[i], recv_sem.at[i]).wait()

    turns = next(b for b in (max(8 // reps, 1), 1) if slots % b == 0)
    sources = [(t, n) for t in range(turns) for n in range(reps)]
    width = len(sources) * per * LANES
    half = jnp.bfloat16
    tall = max(blocks, 16)
    step_ids = lax.broadcasted_iota(jnp.int32, (16, width), 0)

    def rows_of(row):
        return jnp.broadcast_to(row, (16, width)).astype(half)

    def spread(ids, first, count, values):
        masks = [
            (step_ids + (first + r)).astype(jnp.float32).astype(half) == ids
            for r in range(0, count, 16)
        ]
        zero = jnp.zeros((16, width), half)
        return [jnp.where(mask, value, zero) for value in values for mask in masks]

    def measure_all():
        logit = got[:, :, 0]
        label = got[:, :, 2]
        small = jnp.exp(-jnp.abs(logit))
        predicted = jnp.where(logit >= 0.0, 1.0, small) / (1.0 + small)
        vals[:, :, 0] = predicted
        vals[:, :, 1] = jnp.maximum(logit, 0.0) + jnp.log1p(small) - label * logit
        vals[:, :, 2] = (predicted - label) ** 2

    def add(step, carry):
        first = step * turns
        out = []
        for e in range(held):

            def line(ref, k):
                return jnp.concatenate(
                    [
                        ref[first + t, n, k, row : row + 1, :]
                        for t, n in sources
                        for row in range(e * per, (e + 1) * per)
                    ],
                    axis=1,
                )

            bucket = line(got, 1).astype(jnp.int32)
            low = rows_of((bucket & (LANES - 1)).astype(jnp.float32))
            high = rows_of(
                lax.shift_right_logical(bucket, LANES.bit_length() - 1).astype(jnp.float32)
            )
            observed = line(got, 2)
            labels = [rows_of(observed), rows_of(1.0 - observed)]
            values = [rows_of(line(vals, k)) for k in range(3)]
            one_hot = jnp.concatenate(
                spread(low, 0, LANES, [jnp.ones((16, width), half)]), axis=0
            )
            left = jnp.concatenate(
                spread(high, 0, HIGHS, labels) + spread(high, x * blocks, tall, values), axis=0
            )
            out.append(
                carry[e]
                + lax.dot_general(
                    left, one_hot, (((1,), (1,)), ((), ())), preferred_element_type=jnp.float32
                )
            )
        return tuple(out)

    scores(range(pair), True)

    loads["bucket"].wait()
    loads["label"].wait()
    for i in range(intervals):
        for j in range(per):
            c, row = divmod(i * per + j, lines)
            cols = slice(j * LANES, (j + 1) * LANES)
            packed[c, 1, row : row + 1, :] = bucket_ref[i : i + 1, cols].astype(jnp.float32)
            packed[c, 2, row : row + 1, :] = label_ref[i : i + 1, cols].astype(jnp.float32)

    pl.semaphore_wait(barrier, devices - 1)
    for i in range(pair):
        send(i)

    @pl.loop(1, slots // pair)
    def _(step):
        order = [step * pair + p for p in range(pair)]
        scores(order, False)
        for i in order:
            send(i)

    last = slots - 1
    pltpu.make_async_copy(packed.at[slot], got.at[last, here], recv_sem.at[last]).start()
    for i in range(slots):
        arrived(i)
    measure_all()
    zero = jnp.zeros(totals.shape[1:], jnp.float32)
    sums = lax.fori_loop(0, slots // turns, add, (zero,) * held)
    for e in range(held):
        totals[e] = sums[e]

    def below_than(size, lower_first):
        a = lax.broadcasted_iota(jnp.int32, (size, size), 0)
        b = lax.broadcasted_iota(jnp.int32, (size, size), 1)
        return jnp.where(a < b if lower_first else b < a, 1.0, 0.0).astype(jnp.bfloat16)

    lane_before = below_than(LANES, True)
    row_before = below_than(HIGHS, False)
    lane_ids = lax.broadcasted_iota(jnp.int32, (8, LANES), 1)
    bound = devices * per * LANES

    for i in range(held):
        total = totals[i]
        at = slot * held + i
        own = pl.ds(pl.multiple_of(x * blocks, blocks), blocks)
        own_neg = pl.ds(pl.multiple_of(HIGHS + x * blocks, blocks), blocks)
        positives, negatives = totals[i, own, :], totals[i, own_neg, :]
        count = jnp.maximum(positives + negatives, 1.0)
        report = [positives / count]
        for k in range(3):
            first = 2 * HIGHS + k * tall
            report.append(total[first : first + blocks] / count)
        for k in range(4):
            res[at, k : k + 1, 0:span] = jnp.concatenate(
                [report[k][h : h + 1] for h in range(blocks)], axis=1
            )
        pos, neg = total[:HIGHS], total[HIGHS : 2 * HIGHS]
        lane_below = jnp.zeros((HIGHS, LANES), jnp.float32)
        rows_below = jnp.zeros((HIGHS, LANES), jnp.float32)
        for digit, scale in exact_digits(neg, bound):
            digit = digit.astype(jnp.bfloat16)
            lane_below += scale * jnp.dot(
                digit, lane_before, preferred_element_type=jnp.float32
            )
            rows_below += scale * jnp.dot(
                row_before, digit, preferred_element_type=jnp.float32
            )
        below = lane_below + jnp.sum(rows_below, axis=1, keepdims=True)
        sums = [pos * (below + 0.5 * neg), pos, neg]
        sums = [jnp.sum(a, axis=0, keepdims=True) for a in sums]
        for k in range(3):
            part = jnp.sum(vals[:, :, k, i * per : (i + 1) * per, :], axis=(0, 1))
            sums.append(jnp.sum(part, axis=0, keepdims=True))
        sums += [jnp.zeros((1, LANES), jnp.float32)] * 2
        sums = jnp.sum(jnp.concatenate(sums, axis=0), axis=1, keepdims=True)
        numerator, p_sum, n_sum, s_p, s_loss, s_sq = (sums[k : k + 1] for k in range(6))
        examples = jnp.maximum(p_sum + n_sum, 1.0)
        line = jnp.where(lane_ids == 0, numerator / jnp.maximum(p_sum * n_sum, 1.0), 0.0)
        line = jnp.where(lane_ids == 1, s_loss / examples, line)
        line = jnp.where(lane_ids == 2, s_p / jnp.maximum(p_sum, 1.0), line)
        line = jnp.where(lane_ids == 3, s_sq / examples, line)
        res[at, :, span:] = line[0:4]

    own = pl.ds(slot * held, held)

    @pl.loop(1, slots)
    def _(k):
        d = x * group + own_copy * slots + lax.rem(slot + k, slots)
        pltpu.make_async_remote_copy(
            src_ref=res.at[own],
            dst_ref=res.at[own],
            send_sem=res_send_sem,
            recv_sem=res_recv_sem,
            device_id=place(d),
            device_id_type=MESH,
        ).start()

    others = res.at[pl.ds(0, intervals - held)]
    if slots > 1:
        pltpu.make_async_copy(others, others, res_recv_sem).wait()
    reports = pltpu.make_async_copy(res.at[:, :, pl.ds(0, span)], stats_ref, out_sem)
    reports.start()
    pick = jnp.where(
        lax.broadcasted_iota(jnp.int32, (8, LANES), 0)
        == lax.broadcasted_iota(jnp.int32, (8, LANES), 1),
        1.0,
        0.0,
    )
    summary_ref[...] = lax.dot_general(
        pick,
        res[:, 0, span:],
        (((1,), (1,)), ((), ())),
        preferred_element_type=jnp.float32,
        precision=lax.Precision.HIGHEST,
    )[:4]
    reports.wait()
    if slots > 1:
        pltpu.make_async_copy(others, others, res_send_sem).wait()
    for i in range(slots):
        count = reps - 1 if i == last else reps
        if count:
            sent = got.at[i, pl.ds(0, count)]
            pltpu.make_async_copy(sent, sent, send_sem.at[i]).wait()


def finish_kernel(stats_in, summary_in, stats_ref, summary_ref, sems):
    copies = [
        pltpu.make_async_copy(stats_in, stats_ref, sems.at[0]),
        pltpu.make_async_copy(summary_in, summary_ref, sems.at[1]),
    ]
    for copy in copies:
        copy.start()
    for copy in copies:
        copy.wait()


def on_device(sizes, *args):
    (
        interact,
        weight_one,
        bias_one,
        weight_two,
        bias_two,
        weight_three,
        bias_three,
        weight_four,
        bias_four,
        weight_out,
        bias_out,
        bucket_index,
        labels,
    ) = args
    intervals, rows, features = interact.shape
    nx, ny, nz = sizes
    devices = nx * ny * nz
    slots = min(ny * nz, intervals)
    pair = PAIR if slots % PAIR == 0 else 1
    held = intervals // slots
    tile = held * rows
    lines = tile // LANES
    blocks = HIGHS // nx
    reps = devices // slots
    weights = (weight_one, weight_two, weight_three, weight_four)
    operands = [
        interact.reshape(slots, tile, features),
        weight_one,
        bias_one.reshape(1, -1),
        weight_two,
        bias_two.reshape(1, -1),
        weight_three,
        bias_three.reshape(1, -1),
        weight_four,
        bias_four.reshape(1, -1),
        weight_out.reshape(1, -1),
        bias_out,
        bucket_index,
        labels,
    ]
    vmem = pl.BlockSpec(memory_space=pltpu.VMEM)
    in_specs = [pl.BlockSpec(memory_space=pltpu.HBM)] * len(operands)
    in_specs[10] = pl.BlockSpec(memory_space=pltpu.SMEM)
    stats, summary = pl.pallas_call(
        functools.partial(report_kernel, sizes, slots),
        in_specs=in_specs,
        out_specs=[pl.BlockSpec(memory_space=pltpu.HBM), vmem],
        out_shape=[
            jax.ShapeDtypeStruct((intervals, 4, blocks * LANES), jnp.float32),
            jax.ShapeDtypeStruct((4, intervals), jnp.float32),
        ],
        scratch_shapes=[pltpu.VMEM(a.shape, a.dtype) for k, a in enumerate(operands) if k != 10]
        + [pltpu.VMEM((pair, tile, w.shape[1]), jnp.bfloat16) for w in weights]
        + [
            pltpu.VMEM((slots, 3, lines, LANES), jnp.float32),
            pltpu.VMEM((slots, reps, 3, lines, LANES), jnp.float32),
            pltpu.VMEM((slots, reps, 3, lines, LANES), jnp.float32),
            pltpu.VMEM((held, 2 * HIGHS + 3 * max(blocks, 16), LANES), jnp.float32),
            pltpu.VMEM((intervals, 4, (blocks + 1) * LANES), jnp.float32),
            pltpu.SemaphoreType.DMA((slots,)),
            pltpu.SemaphoreType.DMA((11,)),
            pltpu.SemaphoreType.DMA((slots,)),
            pltpu.SemaphoreType.DMA((slots,)),
            pltpu.SemaphoreType.DMA,
            pltpu.SemaphoreType.DMA,
            pltpu.SemaphoreType.DMA,
        ],
        compiler_params=pltpu.CompilerParams(
            collective_id=0, has_side_effects=True, vmem_limit_bytes=60 * 2**20
        ),
        name="report",
    )(*operands)
    hbm = pl.BlockSpec(memory_space=pltpu.HBM)
    stats, summary = pl.pallas_call(
        finish_kernel,
        in_specs=[vmem, vmem],
        out_specs=[hbm, hbm],
        out_shape=[jax.ShapeDtypeStruct(a.shape, a.dtype) for a in (stats, summary)],
        scratch_shapes=[pltpu.SemaphoreType.DMA((2,))],
        compiler_params=pltpu.CompilerParams(vmem_limit_bytes=60 * 2**20),
        name="finish",
    )(stats, summary)
    return stats, summary.T


def solution(mesh):
    sizes = tuple(mesh.shape[a] for a in AXES)
    in_specs = (
        (P(None, AXES, None),) + (P(),) * 10 + (P(None, AXES), P(None, AXES))
    )
    out_specs = (P(None, None, "gx"), P())
    return jax.shard_map(
        functools.partial(on_device, sizes),
        mesh=mesh,
        in_specs=in_specs,
        out_specs=out_specs,
        check_vma=False,
    )
```
